128 devices in a mesh: dp: 4 (over x), row: 2 (over core), col: 16 (over z, y).
Axes of the slice: x: 4, y: 4, z: 4, core: 2. Of those that a mesh axis runs over, the one named last changes fastest.
Arguments:
- block_input: bfloat16 [8192, 2048], P(('dp', 'row'), 'col'), may hold values from -15.5 to 15.5
- gain_attn: bfloat16 [2048], P('col'), may hold values from 0.099609375 to 1.8984375
- w_query: bfloat16 [2048, 2048], P('col', 'row'), may hold values from -0.125 to 0.125
- w_key: bfloat16 [2048, 512], P('col', 'row'), may hold values from -0.125 to 0.125
- w_value: bfloat16 [2048, 512], P('col', 'row'), may hold values from -0.125 to 0.125
- w_out: bfloat16 [2048, 2048], P('row', 'col'), may hold values from -1.5 to 1.5
- gain_mlp: bfloat16 [2048], P('col'), may hold values from 0.099609375 to 1.8984375
- w_gate: bfloat16 [2048, 8192], P('col', 'row'), may hold values from -0.125 to 0.125
- w_up: bfloat16 [2048, 8192], P('col', 'row'), may hold values from -0.125 to 0.125
- w_down: bfloat16 [8192, 2048], P('row', 'col'), may hold values from -0.0625 to 0.0625
- lengths: int32 [4, 7], P('dp'), may hold values from 1 to 512, 2048 in all within a row
- cotangent: bfloat16 [8192, 2048], P(('dp', 'row'), 'col'), may hold values from -6 to 6
Outputs:
- output: bfloat16 [8192, 2048], P(('dp', 'row'), 'col')
- grad_input: float32 [8192, 2048], P(('dp', 'row'), 'col')
- grad_gain_attn: float32 [2048], P('col')
- grad_w_query: float32 [2048, 2048], P('col', 'row')
- grad_w_key: float32 [2048, 512], P('col', 'row')
- grad_w_value: float32 [2048, 512], P('col', 'row')
- grad_w_out: float32 [2048, 2048], P('row', 'col')
- grad_gain_mlp: float32 [2048], P('col')
- grad_w_gate: float32 [2048, 8192], P('col', 'row')
- grad_w_up: float32 [2048, 8192], P('col', 'row')
- grad_w_down: float32 [8192, 2048], P('row', 'col')
The draws below stay inside these ranges and needn't reach their ends.
Inputs may be any that keep to these rules, and one draw needn't show every extreme that they name: Row g holds the lengths of the sequences of data batch g in order; each row sums to 2048 and its largest entry is 512.
All inputs are finite; a program needn't handle non-finite values.
Results may differ from the reference program's by a relative error of at most 0.02.
Values may be sent and summed in bfloat16 or wider, within the bound.
A program may use at most 192 MiB of HBM per device.

```python
import math
import jax
import jax.numpy as jnp
import numpy as np
from jax import lax

D = 2048
FF = 8192
HQ = 32
HK = 8
HS = 64
LONGEST = 512
TOK_GROUP = 2048
SEQS = 7
TOKENS = 8192
N_DP = 4


def draw_block_input(key, part):
    key = jax.random.fold_in(key, 11)
    pick_key, level_key, base_key = jax.random.split(key, 3)
    picked_total = max(1, D // 256)
    ranks = jax.random.permutation(pick_key, D)
    picked = ranks < picked_total
    signs_row = jnp.where(ranks % 2 == 0, 1.0, -1.0).astype(jnp.float32)
    base = jnp.clip(jax.random.normal(base_key, (TOKENS, D), jnp.float32), -6.0, 6.0)
    height = math.sqrt(0.4 * D / picked_total)
    spread_rows = jax.random.uniform(level_key, (TOKENS, D), jnp.float32, 0.75, 1.25)
    values = jnp.where(picked[None, :], signs_row[None, :] * height * spread_rows, base)
    return values.astype(jnp.bfloat16)


def block_levels(rng, dims, pieces, least, largest):
    gain, own = 1.0, jax.random.fold_in(rng, 6)
    for dim, shards_of in pieces:
        heights = jnp.exp(jax.random.uniform(jax.random.fold_in(own, dim), (shards_of,), jnp.float32, least / len(pieces), largest / len(pieces)))
        gain = gain * jnp.repeat(heights, dims[dim] // shards_of).reshape([-1 if axis == dim else 1 for axis in range(len(dims))])
    return gain


def length_profile(count, total, reach, slope):
    loads = [(1 << 20) // math.isqrt(rank ** slope) + 1 for rank in range(2, count + 1)]
    spare, holding = total - reach - (count - 1), [1] * (count - 1)
    while spare > 0:
        free = [i for i in range(count - 1) if holding[i] < reach]
        whole, budget = sum([loads[i] for i in free]), spare
        for i in free:
            extra = min(reach - holding[i], max(1, budget * loads[i] // whole), spare)
            holding[i] = holding[i] + extra
            spare = spare - extra
    return np.array([reach] + holding)


def ragged(stream_key, number_of, total, limit, skew):
    if number_of == 2:
        one = jax.random.randint(stream_key, (), max(1, total - limit), min(limit, total - 1) + 1)
        return jnp.stack([one, total - one])
    sizes = jnp.asarray(length_profile(number_of, total, limit, skew), jnp.int32)
    pairs = (number_of - 1) // 2
    source_of, sink = sizes[1:1 + 2 * pairs:2], sizes[2:2 + 2 * pairs:2]
    margin = jnp.minimum(source_of - 1, limit - sink)
    shifted = jax.random.randint(jax.random.fold_in(stream_key, 1), (pairs,), 0, 1 << 20) % (margin + 1)
    sizes = sizes.at[1:1 + 2 * pairs:2].set(source_of - shifted).at[2:2 + 2 * pairs:2].set(sink + shifted)
    return sizes[jax.random.permutation(jax.random.fold_in(stream_key, 2), number_of)]


def noise(rng, dims, scale, bound, shards=(), kind=jnp.bfloat16):
    array = jax.random.normal(rng, dims, jnp.float32) * scale
    if len(shards) > 0:
        array = block_levels(rng, dims, shards, -0.22, 0.18) * array
    return jnp.clip(array, min=-bound, max=bound).astype(kind)


def setup_inputs(seed: int = 0) -> dict:
    streams_of = jax.random.split(jax.random.key(seed), 13)
    block_input = draw_block_input(jax.random.fold_in(streams_of[12], 71), 0)
    gain_attn = jnp.clip(1.0 + 0.18 * jax.random.normal(streams_of[1], (D,), jnp.float32), 0.099609375, 1.8984375).astype(jnp.bfloat16)
    w_query = noise(streams_of[2], (D, HQ * HS), D ** -0.5, 0.125, ((0, 16), (1, 2)))
    w_key = noise(streams_of[3], (D, HK * HS), D ** -0.5, 0.125, ((0, 16), (1, 2)))
    w_value = noise(streams_of[4], (D, HK * HS), D ** -0.5, 0.125, ((0, 16), (1, 2)))
    w_out = noise(streams_of[5], (HQ * HS, D), (HQ * HS // 128) ** -0.5, 1.5, ((0, 2), (1, 16)))
    gain_mlp = jnp.clip(1.0 + 0.18 * jax.random.normal(streams_of[6], (D,), jnp.float32), 0.099609375, 1.8984375).astype(jnp.bfloat16)
    w_gate = noise(streams_of[7], (D, FF), D ** -0.5, 0.125, ((0, 16), (1, 2)))
    w_up = noise(streams_of[8], (D, FF), D ** -0.5, 0.125, ((0, 16), (1, 2)))
    w_down = noise(streams_of[9], (FF, D), FF ** -0.5, 0.0625, ((0, 2), (1, 16)))
    lengths = jax.vmap(lambda own: ragged(own, SEQS, TOK_GROUP, LONGEST, 2))(jax.random.split(streams_of[10], N_DP)).reshape((N_DP, SEQS)).astype(jnp.int32)
    cotangent = noise(streams_of[11], (TOKENS, D), 1.0, 6.0, ((0, 8), (1, 16)))
    return dict(block_input=block_input, gain_attn=gain_attn, w_query=w_query, w_key=w_key, w_value=w_value, w_out=w_out, gain_mlp=gain_mlp, w_gate=w_gate, w_up=w_up, w_down=w_down, lengths=lengths, cotangent=cotangent)


EPS = 1e-05
THETA = 500000.0
HIGH = lax.Precision.HIGHEST

@jax.custom_vjp
def low(v):
    return lax.optimization_barrier(v.astype(jnp.bfloat16)).astype(jnp.float32)

@jax.custom_vjp
def low_back(v):
    return v

def low_keep(v):
    return (low(v), None)

def low_pass(kept, grad):
    return (grad,)

def back_keep(v):
    return (v, None)

def back_low(kept, grad):
    return (low(grad),)
low.defvjp(low_keep, low_pass)
low_back.defvjp(back_keep, back_low)

def layout(lengths, count):
    lens = lengths.reshape(-1).astype(jnp.int32)
    ends = jnp.cumsum(lens).astype(jnp.int32)
    starts = (ends - lens).astype(jnp.int32)
    places = jnp.arange(count, dtype=jnp.int32)
    began = starts[None, :] <= places[:, None]
    segment = (lax.optimization_barrier(jnp.sum(began.astype(jnp.int32), axis=1)) - 1).astype(jnp.int32)
    offset = lax.optimization_barrier(jnp.max(jnp.where(began, starts[None, :], 0), axis=1)).astype(jnp.int32)
    return ((places - offset).astype(jnp.int32), segment)

def angles(places, half):
    freqs = THETA ** (-(jnp.arange(half, dtype=jnp.float32) * 2.0) / (2.0 * half))
    turned = places.astype(jnp.float32)[:, None] * freqs[None, :]
    return (jnp.cos(turned)[:, None, :], jnp.sin(turned)[:, None, :])

def rotate(values, cosine, sine):
    half = cosine.shape[-1]
    first = values[..., :half]
    second = values[..., half:]
    return jnp.concatenate([first * cosine - second * sine, second * cosine + first * sine], axis=-1)

def masks(segment, first, lower, block, window):
    seg_query = lax.dynamic_slice_in_dim(segment, first, block, 0)
    seg_key = lax.dynamic_slice_in_dim(segment, lower, window, 0)
    mark_query = first + jnp.arange(block, dtype=jnp.int32)
    mark_key = lower + jnp.arange(window, dtype=jnp.int32)
    return (seg_query[:, None] == seg_key[None, :]) & (mark_key[None, :] <= mark_query[:, None])

def matmul(left, right):
    return jnp.dot(left, right, precision=HIGH)

def rms_scale(values):
    return lax.rsqrt(lax.optimization_barrier(jnp.mean(values * values, axis=1, keepdims=True)) + EPS)

def attend(queries, keys, values, segment):
    group = queries.shape[0]
    block = min(512, group)
    window = min(group, block + LONGEST)
    repeat = HQ // HK
    scale = HS ** (-0.5)

    def one_block(first):
        lower = jnp.clip(first + block - window, 0, group - window).astype(jnp.int32)
        query_blk = lax.dynamic_slice_in_dim(queries, first, block, 0)
        key_win = jnp.repeat(lax.dynamic_slice_in_dim(keys, lower, window, 0), repeat, axis=1)
        value_win = jnp.repeat(lax.dynamic_slice_in_dim(values, lower, window, 0), repeat, axis=1)
        scores = low_back(jnp.einsum('qhd,khd->hqk', query_blk, key_win, precision=HIGH) * scale)
        allowed = masks(segment, first, lower, block, window)
        probs = jax.nn.softmax(jnp.where(allowed[None], scores, -1e+30), axis=-1)
        return jnp.einsum('hqk,khd->qhd', low(probs), value_win, precision=HIGH)
    firsts = (jnp.arange(group // block) * block).astype(jnp.int32)
    outputs = lax.map(jax.checkpoint(one_block), firsts)
    return outputs.reshape(group, HQ * HS)

def forward(input_rows, attention_gain, w_query, w_key, w_value, w_out, feedforward_gain, w_gate, w_up, w_down, cosine, sine, segment):
    group = input_rows.shape[0]
    normed_one = low(input_rows * rms_scale(input_rows) * attention_gain)
    queries = low(rotate(low_back(matmul(normed_one, w_query)).reshape(group, HQ, HS), cosine, sine))
    keys = low(rotate(low_back(matmul(normed_one, w_key)).reshape(group, HK, HS), cosine, sine))
    values = low(low_back(matmul(normed_one, w_value))).reshape(group, HK, HS)
    heads = low(low_back(attend(queries, keys, values, segment)))
    hidden_after_attention = input_rows + low_back(matmul(heads, w_out))
    normed_two = low(hidden_after_attention * rms_scale(hidden_after_attention) * feedforward_gain)
    gate = low_back(matmul(normed_two, w_gate))
    up = low_back(matmul(normed_two, w_up))
    act = low(jax.nn.silu(gate) * up)
    return hidden_after_attention + low_back(matmul(act, w_down))

def reference(block_input, gain_attn, w_query, w_key, w_value, w_out, gain_mlp, w_gate, w_up, w_down, lengths, cotangent):
    weights = tuple((w.astype(jnp.float32) for w in (gain_attn, w_query, w_key, w_value, w_out, gain_mlp, w_gate, w_up, w_down)))
    input_rows = block_input.astype(jnp.float32).reshape(N_DP, TOK_GROUP, D)
    grads_in = cotangent.astype(jnp.float32).reshape(N_DP, TOK_GROUP, D)

    def one_batch(totals, item):
        batch, grad_batch, lens = item
        places, segment = layout(lens, TOK_GROUP)
        cosine, sine = angles(places, HS // 2)

        def apply_block(inputs_f, *params):
            return forward(inputs_f, *params, cosine, sine, segment)
        result, pull = jax.vjp(apply_block, batch, *weights)
        grads = pull(grad_batch)
        totals = tuple((total + grad for total, grad in zip(totals, grads[1:])))
        return (totals, (result.astype(jnp.bfloat16), grads[0]))
    start_sums = tuple((jnp.zeros_like(w) for w in weights))
    sums, (results, grad_inputs) = lax.scan(one_batch, start_sums, (input_rows, grads_in, lengths))
    return (results.reshape(TOKENS, D), grad_inputs.reshape(TOKENS, D), sums[0], sums[1], sums[2], sums[3], sums[4], sums[5], sums[6], sums[7], sums[8])
```

```python
import types

import jax
import jax.numpy as jnp
from jax import lax
from jax.experimental import pallas as pl
from jax.experimental.pallas import tpu as pltpu
from jax.sharding import PartitionSpec as P

HQ = 32
HK = 8
HS = 64
LONGEST = 512
EPS = 1e-05
THETA = 500000.0
MESH = pl.DeviceIdType.MESH
SIDE = 4
COLS = SIDE * SIDE
WIDE = 128
DEEP = SIDE * WIDE
QB = 256
WIN = QB + LONGEST
HEADS = HQ // SIDE
KVS = HK // SIDE
HEAD_WIDTH = (HEADS + 2 * KVS) * HS
MIB = 1024 * 1024
BF16, F32 = jnp.bfloat16, jnp.float32


def spot():
    me = lax.axis_index("col")
    return lax.div(me, SIDE), lax.rem(me, SIDE)


def wrap(value):
    return lax.rem(value + SIDE, SIDE)


def off(place, offset):
    return wrap(place[0] + offset[0]), wrap(place[1] + offset[1])


def at(place, dz, dy):
    z, y = off(place, (dz, dy))
    return {"col": z * SIDE + y}


def shift(axis, amount):
    return (amount, 0) if axis == "z" else (0, amount)


def plus(one, two):
    return one[0] + two[0], one[1] + two[1]


def other_core():
    return {"row": 1 - lax.axis_index("row")}


def beside(step):
    return {"dp": wrap(lax.axis_index("dp") + step)}


def chip(step):
    return lax.rem(lax.axis_index("col") + step + COLS, COLS)


def tile_peer(place, step):
    tile = lax.rem(lax.axis_index("row") * SIDE + place[0] + step + 2 * SIDE, 2 * SIDE)
    return {"col": lax.rem(tile, SIDE) * SIDE + place[1], "row": lax.div(tile, SIDE)}


def hail(place, wide=False):
    barrier = pltpu.get_barrier_semaphore()
    if wide:
        peers = [{"col": chip(k)} for k in range(1, COLS)]
        peers += [beside(k) for k in range(1, SIDE)] + [other_core()]
        peers += [tile_peer(place, k) for k in (1, 2, -1, -2)]
    else:
        peers = [at(place, *shift(axis, step)) for axis in ("z", "y") for step in (1, -1, 2)]
    for peer in peers:
        pl.semaphore_signal(barrier, inc=1, device_id=peer, device_id_type=MESH)
    return len(peers)


def meet(count):
    pl.semaphore_wait(pltpu.get_barrier_semaphore(), count)


def span(block, size):
    return pl.ds(pl.multiple_of(block * size, size), size)


class Plan:
    def __init__(self, words):
        self.words = list(words)
        self.flows = {}

    def add(self, letter, flow):
        self.flows[letter] = flow

    def step(self, letter):
        next(self.flows[letter], None)

    def point(self):
        if self.words:
            for letter in self.words.pop(0):
                self.step(letter)

    def drain(self, letters):
        for letter in letters:
            for _ in self.flows[letter]:
                pass


class Copies:
    def __init__(self, send, recv):
        self.send, self.recv, self.count = send, recv, 0
        self.open = []

    def to(self, peer, source, target):
        copy = pltpu.make_async_remote_copy(
            src_ref=source,
            dst_ref=target,
            send_sem=self.send.at[self.count],
            recv_sem=self.recv.at[self.count],
            device_id=peer,
            device_id_type=MESH,
        )
        self.count += 1
        copy.start()
        self.open.append(copy)
        return copy

    def finish(self):
        for copy in self.open:
            copy.wait_send()


class Locals:
    def __init__(self, sems):
        self.sems, self.open = sems, []

    def move(self, source, target):
        copy = pltpu.make_async_copy(source, target, self.sems.at[len(self.open)])
        copy.start()
        self.open.append(copy)
        return copy


class Slabs:
    def __init__(self, rows):
        self.rows = rows

    def lines(self, half, piece):
        size = self.rows // 2
        if piece is None:
            return half * size, size
        return half * size + piece * (size // 2), size // 2

    def part(self, ref, spot_of, half, piece):
        z, y = spot_of
        return ref.at[pl.ds(*self.lines(half, piece)), span(y * SIDE + z, WIDE)]


class Tiles:
    def __init__(self, first, tall):
        self.first, self.tall = first, tall

    def lines(self, half, piece):
        size = self.tall // 2
        if piece is None:
            return self.first + half * size, size
        return self.first + half * size + piece * (size // 2), size // 2

    def part(self, ref, spot_of, half, piece):
        z, y = spot_of
        first, count = self.lines(half, piece)
        start = pl.multiple_of(z * QB + first, count)
        return ref.at[pl.ds(start, count), span(y, DEEP)]


AXES = (("y", "z"), ("z", "y"))


class Gather:
    COUNT = 40

    def __init__(self, place, full, blocks, send, recv, own=None):
        self.place, self.full, self.blocks = place, full, blocks
        self.send, self.recv, self.own = send, recv, own
        self.copies = []
        self.waited = set()
        self.table = {}

    def _part(self, offset, half, piece):
        return self.blocks.part(self.full, off(self.place, offset), half, piece)

    def _send(self, half, axis, sign, offset, piece):
        index = len(self.copies)
        move = shift(axis, sign)
        block = self._part(offset, half, piece)
        source = block
        if offset == (0, 0) and self.own is not None:
            source = self.own.at[pl.ds(*self.blocks.lines(half, piece)), :]
        copy = pltpu.make_async_remote_copy(
            src_ref=source,
            dst_ref=block,
            send_sem=self.send.at[index],
            recv_sem=self.recv.at[index],
            device_id=at(self.place, *move),
            device_id_type=MESH,
        )
        copy.start()
        self.copies.append(copy)
        landed = (offset[0] - move[0], offset[1] - move[1])
        norm = tuple(2 if v == -2 else v for v in landed)
        self.table.setdefault((half, norm), []).append((index, landed, piece))

    def need(self, half, offset):
        for index, landed, piece in self.table.get((half, offset), ()):
            if index in self.waited:
                continue
            self.waited.add(index)
            block = self._part(landed, half, piece)
            pltpu.make_async_remote_copy(
                src_ref=block,
                dst_ref=block,
                send_sem=self.send.at[index],
                recv_sem=self.recv.at[index],
                device_id=at(self.place, 0, 1),
                device_id_type=MESH,
            ).wait_recv()

    def steps(self):
        for half, (a, b) in enumerate(AXES):
            for sign in (1, -1):
                self._send(half, a, sign, (0, 0), None)
        for half, (a, b) in enumerate(AXES):
            for sign in (1, -1):
                self._send(half, b, sign, (0, 0), None)
        yield 0
        for half, (a, b) in enumerate(AXES):
            for sign in (1, -1):
                offset = shift(a, -sign)
                self.need(half, offset)
                self._send(half, a, sign, offset, 0 if sign == 1 else 1)
                for along in (1, -1):
                    self._send(half, b, along, offset, None)
        yield 1
        for half, (a, b) in enumerate(AXES):
            for sign in (1, -1):
                offset = shift(b, -sign)
                self.need(half, offset)
                self._send(half, b, sign, offset, 0 if sign == 1 else 1)
        yield 2
        for half, (a, b) in enumerate(AXES):
            offset = shift(a, 2)
            self.need(half, offset)
            for along in (1, -1):
                self._send(half, b, along, offset, None)
        yield 3
        for half, (a, b) in enumerate(AXES):
            for o in (1, -1):
                for sign in (1, -1):
                    offset = plus(shift(a, o), shift(b, -sign))
                    self.need(half, offset)
                    self._send(half, b, sign, offset, 0 if sign == 1 else 1)
        yield 4
        for half, (a, b) in enumerate(AXES):
            for sign in (1, -1):
                offset = plus(shift(a, 2), shift(b, -sign))
                self.need(half, offset)
                self._send(half, b, sign, offset, 0 if sign == 1 else 1)
        yield 5

    def finish(self):
        for half, offset in list(self.table):
            self.need(half, offset)
        for copy in self.copies:
            copy.wait_send()


class Scatter:
    COUNT = 40

    def __init__(self, place, part, blocks, halves, quarters, send, recv):
        self.place, self.part, self.blocks = place, part, blocks
        self.halves, self.quarters, self.send, self.recv = halves, quarters, send, recv
        self.copies = []
        self.counts = [0, 0]
        self.landed = {}
        self.results = []

    def _here(self, offset, half, piece):
        return self.blocks.part(self.part, off(self.place, offset), half, piece)

    def _send(self, half, axis, sign, offset, piece, key):
        index = len(self.copies)
        kind = 0 if piece is None else 1
        land = (self.halves if kind == 0 else self.quarters).at[self.counts[kind]]
        self.counts[kind] += 1
        copy = pltpu.make_async_remote_copy(
            src_ref=self._here(offset, half, piece),
            dst_ref=land,
            send_sem=self.send.at[index],
            recv_sem=self.recv.at[index],
            device_id=at(self.place, *shift(axis, sign)),
            device_id_type=MESH,
        )
        copy.start()
        self.copies.append(copy)
        self.landed[key] = (copy, land)

    def _take(self, key):
        copy, land = self.landed[key]
        copy.wait_recv()
        return land[...]

    def _three(self, half, offset, name):
        summed = self._here(offset, half, None)[...].astype(F32)
        there = self._take((name, half, 1, "h")).astype(F32)
        return summed + (there + self._take((name, half, -1, "h")).astype(F32))

    def _line(self, half, axis, base, name):
        for sign in (1, -1):
            offset = plus(base, shift(axis, 2 * sign))
            piece = 0 if sign == 1 else 1
            self._send(half, axis, sign, offset, piece, (name, half, sign, "q"))

    def _pass(self, half, axis, base, name):
        for sign in (1, -1):
            offset = plus(base, shift(axis, sign))
            here = self._here(offset, half, 0 if sign == 1 else 1)
            here[...] = here[...] + self._take((name, half, sign, "q"))
            self._send(half, axis, sign, offset, None, (name, half, sign, "h"))

    def steps(self):
        outer = (2, 1, -1, 0)
        for o in outer:
            for half, (a, b) in enumerate(AXES):
                self._line(half, b, shift(a, o), o)
        yield 0
        for o in outer:
            for half, (a, b) in enumerate(AXES):
                self._pass(half, b, shift(a, o), o)
            yield 1
        for half, (a, b) in enumerate(AXES):
            summed = self._three(half, shift(a, 2), 2)
            self._here(shift(a, 2), half, None)[...] = summed.astype(BF16)
            self._line(half, a, (0, 0), "own")
        yield 2
        for half, (a, b) in enumerate(AXES):
            for sign in (1, -1):
                summed = self._three(half, shift(a, sign), sign)
                self._here(shift(a, sign), half, None)[...] = summed.astype(BF16)
        yield 3
        for half, (a, b) in enumerate(AXES):
            self._pass(half, a, (0, 0), "own")
        yield 4
        for half, (a, b) in enumerate(AXES):
            summed = self._three(half, (0, 0), 0)
            there = self._take(("own", half, 1, "h")).astype(F32)
            there = there + self._take(("own", half, -1, "h")).astype(F32)
            self.results.append((self.blocks.lines(half, None), summed + there))
        yield 5

    def finish(self):
        for copy in self.copies:
            copy.wait_send()


class Along:
    def __init__(self, axis, place=None):
        self.axis, self.place = axis, place
        self.me = lax.axis_index("dp") if axis == "dp" else place["zy".index(axis)]

    def peer(self, step):
        if self.axis == "dp":
            return beside(step)
        return at(self.place, *shift(self.axis, step))

    def pos(self, step):
        return wrap(self.me + step)


class RingGather:
    def __init__(self, copies, along, pieces):
        self.copies, self.along, self.pieces = copies, along, pieces

    def start(self):
        along = self.along
        self.first = [
            [self.copies.to(along.peer(s), p, p) for p in self.pieces(along.me, None)]
            for s in (1, -1)
        ]

    def relay(self, arrived=None):
        along = self.along
        self.second = []
        for n, s in enumerate((1, -1)):
            for copy in self.first[n]:
                copy.wait_recv()
            came = along.pos(-s)
            self.second += [self.copies.to(along.peer(s), p, p) for p in self.pieces(came, n)]
            if arrived is not None:
                arrived(came)

    def finish(self, arrived=None):
        for copy in self.second:
            copy.wait_recv()
        if arrived is not None:
            arrived(self.along.pos(2))


class RingScatter:
    def __init__(self, copies, along, pieces, halves, fulls):
        self.copies, self.along, self.pieces = copies, along, pieces
        self.halves, self.fulls = halves, fulls

    def start(self):
        along = self.along
        self.first = [
            [
                self.copies.to(along.peer(s), p, land)
                for p, land in zip(self.pieces(along.pos(2), n), self.halves[n], strict=True)
            ]
            for n, s in enumerate((1, -1))
        ]

    def relay(self):
        along = self.along
        self.second = []
        for n, s in enumerate((1, -1)):
            targets = self.pieces(along.pos(s), n)
            for copy, target, land in zip(self.first[n], targets, self.halves[n], strict=True):
                copy.wait_recv()
                target[...] = target[...] + land[...]
            for p, land in zip(self.pieces(along.pos(s), None), self.fulls[n], strict=True):
                self.second.append(self.copies.to(along.peer(s), p, land))

    def wait(self):
        for copy in self.second:
            copy.wait_recv()

    def total(self, index=0):
        there = self.fulls[0][index][...].astype(F32) + self.fulls[1][index][...].astype(F32)
        return self.pieces(self.along.me, None)[index][...].astype(F32) + there


class AxisTotals:
    def __init__(self, place, own, slots, send, recv):
        self.own, self.slots = own, slots
        self.copies = Copies(send, recv)
        for i, step in enumerate((1, -1, 2)):
            self.copies.to(at(place, 0, step), own, slots.at[i])

    def finish(self):
        for copy in self.copies.open:
            copy.wait_recv()
        self.copies.finish()
        return (self.own[...] + self.slots[2]) + (self.slots[0] + self.slots[1])


class Totals:
    def __init__(self, place, own, mid, slots, send, recv):
        self.place, self.own, self.mid, self.slots = place, own, mid, slots
        self.send, self.recv = send, recv
        self.open = []

    def _start(self, axis, source, base):
        for i, step in enumerate((1, -1, 2)):
            copy = pltpu.make_async_remote_copy(
                src_ref=source,
                dst_ref=self.slots.at[base + i],
                send_sem=self.send.at[base + i],
                recv_sem=self.recv.at[base + i],
                device_id=at(self.place, *shift(axis, step)),
                device_id_type=MESH,
            )
            copy.start()
            self.open.append(copy)

    def first(self):
        self._start("y", self.own, 0)

    def second(self):
        for copy in self.open[:3]:
            copy.wait_recv()
        self.mid[...] = (self.own[...] + self.slots[2]) + (self.slots[0] + self.slots[1])
        self._start("z", self.mid, 3)

    def finish(self):
        for copy in self.open[3:]:
            copy.wait_recv()
        total = (self.mid[...] + self.slots[5]) + (self.slots[3] + self.slots[4])
        for copy in self.open:
            copy.wait_send()
        return total


def nt(left, right):
    return lax.dot_general(left, right, (((1,), (1,)), ((), ())), preferred_element_type=F32)


def tn(left, right):
    return lax.dot_general(left, right, (((0,), (0,)), ((), ())), preferred_element_type=F32)


def nn(left, right):
    return jnp.dot(left, right, preferred_element_type=F32)


def lane(shape):
    return lax.broadcasted_iota(jnp.int32, shape, 1)


def turn(values, cosine, sine):
    width = values.shape[1]
    half = HS // 2
    other = jnp.where(
        lane(values.shape) % HS < half,
        pltpu.roll(values, width - half, 1),
        pltpu.roll(values, half, 1),
    )
    return values * cosine + other * sine


def row_sums(values):
    ones = jnp.ones((8, values.shape[1]), F32)
    return lax.dot_general(
        ones,
        values,
        (((1,), (1,)), ((), ())),
        precision=lax.Precision.HIGHEST,
        preferred_element_type=F32,
    )


def gain_row(gains, which):
    return jnp.concatenate([gains[k][which : which + 1] for k in range(SIDE)], axis=1)


VMEM = pl.BlockSpec(memory_space=pltpu.VMEM)
SMEM = pl.BlockSpec(memory_space=pltpu.SMEM)
ANY = pl.BlockSpec(memory_space=pl.ANY)


def dma(count):
    return pltpu.SemaphoreType.DMA((count,))


def shape(dims, dtype=BF16):
    return jax.ShapeDtypeStruct(dims, dtype)


def launch(kernel, ident, inputs, outs, scratch):
    names = list(inputs) + list(outs) + list(scratch)

    def body(*refs):
        kernel(types.SimpleNamespace(**dict(zip(names, refs, strict=True))))

    results = pl.pallas_call(
        body,
        out_shape=tuple(out for out, _ in outs.values()),
        in_specs=[spec for _, spec in inputs.values()],
        out_specs=tuple(spec for _, spec in outs.values()),
        scratch_shapes=list(scratch.values()),
        compiler_params=pltpu.CompilerParams(
            collective_id=ident, has_side_effects=True, vmem_limit_bytes=60 * MIB
        ),
        name=kernel.__name__,
    )(*(array for array, _ in inputs.values()))
    return types.SimpleNamespace(**dict(zip(outs, results, strict=True)))


def allowed(start):
    key = lax.broadcasted_iota(jnp.int32, (QB, WIN), 1)
    query = LONGEST + lax.broadcasted_iota(jnp.int32, (QB, WIN), 0)
    return (key >= start) & (key <= query)


def probabilities(query, keys, ok):
    scores = jnp.where(ok, nt(query, keys) * HS**-0.5, -1e30)
    expo = jnp.exp(scores - jnp.max(scores, axis=1, keepdims=True))
    return expo * (1.0 / jnp.sum(expo, axis=1, keepdims=True))


def attend_pair(r, j):
    ok = allowed(r.start[...])
    window = r.kvs[lax.div(j, 2)]
    keys, values = window[:, :HS], window[:, HS:]
    queries = r.q[:, span(j, WIDE)]
    both = []
    for h in range(2):
        probs = probabilities(queries[:, h * HS : (h + 1) * HS], keys, ok).astype(BF16)
        both.append(nn(probs, values))
    r.heads[:, span(j, WIDE)] = jnp.concatenate(both, axis=1).astype(BF16)


def attend_pair_back(r, j):
    ok = allowed(r.start[...])
    side = lax.div(j, 2)
    window = r.kvs[side]
    keys, values = window[:, :HS], window[:, HS:]
    queries, grads = r.q[:, span(j, WIDE)], r.gheads[:, span(j, WIDE)]
    both = []
    key_sum = value_sum = None
    for h in range(2):
        query, grad = queries[:, h * HS : (h + 1) * HS], grads[:, h * HS : (h + 1) * HS]
        probs = probabilities(query, keys, ok)
        grad_probs = nt(grad, values)
        delta = jnp.sum(probs * grad_probs, axis=1, keepdims=True)
        grad_scores = (probs * (grad_probs - delta)).astype(BF16)
        both.append(nn(grad_scores, keys) * HS**-0.5)
        key_term = tn(grad_scores, query) * HS**-0.5
        value_term = tn(probs.astype(BF16), grad)
        key_sum = key_term if h == 0 else key_sum + key_term
        value_sum = value_term if h == 0 else value_sum + value_term
    r.dq[:, span(j, WIDE)] = jnp.concatenate(both, axis=1)
    r.dkv[side] = r.dkv[side] + jnp.concatenate([key_sum, value_sum], axis=1)


def out_weights(r, n):
    return jnp.concatenate([r.w_out[n, k].reshape(-1, WIDE) for k in range(SIDE)], axis=1)


AHEAD_PLAN = (
    "owkow",
    "",
    "o",
    "b",
    "",
    "wcow",
    "ao",
    "",
    "",
    "ock",
    "",
    "akb",
    "",
    "",
    "",
    "ka",
    "k",
    "ak",
    "1c21",
    "21b1",
    "",
    "12a",
    "bc1",
    "22",
    "",
    "2",
    "",
    "",
    "3",
    "33",
    "33",
    "3",
    "4",
    "f4e43",
    "44ff43e",
    "4e",
    "4ef",
)


def front(r, place, plan, local):
    z, y = place
    core = lax.axis_index("row")
    quarter = lax.axis_index("dp")
    depth = r.wg.shape[0]
    width = COLS * depth
    unit = r.wd.shape[0] // COLS
    share, tall = depth // SIDE, unit // SIDE
    half = depth // 2
    strip = r.strips.shape[1]
    nq, nk = r.wq.shape[1], r.wk.shape[1]
    count = hail(place, wide=True)
    misc, deals, flows = Copies(r.ms, r.mr), Copies(r.bs, r.br), Copies(r.ws, r.wr)
    spot_of = y * SIDE + z
    along_y, along_z, along_dp = Along("y", place), Along("z", place), Along("dp")

    def dealt(ref, which):
        return ref.at[span(which, half), :]

    def dealt_out(n, which):
        first = n * (r.wo.shape[0] // 2) + (quarter * 2 + which) * strip
        return r.wo.at[pl.ds(pl.multiple_of(first, strip), strip), :]

    parts = ((r.wq, 0, nq), (r.wk, nq, nk), (r.wv, nq + nk, nk))
    kept = [
        local.move(dealt(ref, core), r.mine.at[:, pl.ds(first, size)])
        for ref, first, size in parts
    ]
    kept_x = local.move(r.x.at[span(z, QB), :], r.xt.at[:, span(z, WIDE)])
    kept_out = [local.move(dealt_out(n, core), r.strips.at[2 * core + n]) for n in range(2)]
    kept_cot = local.move(r.cot, r.cots.at[:, span(spot_of, WIDE)])
    row = lax.broadcasted_iota(jnp.int32, (8, WIDE), 0)
    one = r.gain_one[...].astype(F32).reshape(1, WIDE)
    two = r.gain_two[...].astype(F32).reshape(1, WIDE)
    r.gains[z] = jnp.where(row == 0, one, two)
    meet(count)
    swaps = [
        misc.to(other_core(), dealt(ref, 1 - core), r.theirs.at[:, pl.ds(first, size)])
        for ref, first, size in parts
    ]
    x_moves = []
    for k in (1, -1, 2):
        to = wrap(z + k)
        x_moves.append(
            misc.to(at(place, k, 0), r.x.at[span(to, QB), :], r.xt.at[:, span(z, WIDE)])
        )
        x_moves.append(misc.to(at(place, k, 0), r.gains.at[z], r.gains.at[z]))
    out_swaps = [
        misc.to(other_core(), dealt_out(n, 1 - core), r.strips.at[2 * core + n]) for n in range(2)
    ]

    def gate_cut(ref, chips, pos):
        return ref.at[core, chips, pos, :, pl.ds(0, unit)]

    def up_cut(ref, chips, pos):
        return ref.at[core, chips, pos, :, pl.ds(unit, unit)]

    def cross(pieces):
        return [misc.to(other_core(), p, p) for p in pieces]

    def spread(ring, pieces, me):
        crossing = []
        arrived = lambda pos: crossing.extend(cross(pieces(pos, None)))
        ring.start()
        arrived(me)
        yield 1
        ring.relay(arrived)
        yield 2
        ring.finish(arrived)
        yield 3
        for copy in crossing:
            copy.wait_recv()
        yield 4

    def feed_flow(which):
        waits = []
        mine_rows = span(quarter, share)
        for k in range(COLS):
            to = chip(k)
            if which == 0:
                source = r.wg.at[mine_rows, span(to, unit)]
                target = gate_cut(r.gu, spot_of, quarter)
            elif which == 1:
                source = r.wu.at[mine_rows, span(to, unit)]
                target = up_cut(r.gu, spot_of, quarter)
            else:
                down_rows = pl.ds(pl.multiple_of(to * unit + quarter * tall, tall), tall)
                source = r.wd.at[down_rows, :]
                target = r.d.at[core, quarter, :, span(spot_of, depth)]
            if k == 0:
                waits.append(local.move(source, target).wait)
            else:
                waits.append(deals.to({"col": to}, source, target).wait_recv)
        yield 0

        def pieces(pos, part):
            chips = pl.ds(0, COLS) if part is None else pl.ds(part * (COLS // 2), COLS // 2)
            if which == 0:
                return [gate_cut(r.gu, chips, pos)]
            if which == 1:
                return [up_cut(r.gu, chips, pos)]
            rows = pl.ds(0, tall) if part is None else pl.ds(part * (tall // 2), tall // 2)
            return [r.d.at[core, pos, rows, :]]

        for wait in waits:
            wait()
        yield from spread(RingGather(flows, along_dp, pieces), pieces, quarter)

    def multicast(blocks, ref):
        sends = [
            misc.to(at(place, 0, k), blocks.at[wrap(y + k)], ref.at[y, z, quarter, core])
            for k in (1, -1, 2)
        ]
        ref[y, z, quarter, core] = blocks[y]
        yield 0
        for copy in sends:
            copy.wait_recv()

        def lead(part):
            return pl.ds(0, SIDE) if part is None else pl.ds(part * 2, 2)

        ring = RingGather(
            misc, along_z, lambda pos, part: [ref.at[lead(part), pos, quarter, core]]
        )
        ring.start()
        yield 1
        ring.relay()
        yield 2
        ring.finish()
        pieces = lambda pos, part: [ref.at[lead(part), :, pos, core]]
        yield from spread(RingGather(misc, along_dp, pieces), pieces, quarter)

    def head_flow():
        for copy in kept:
            copy.wait()
        for copy in swaps:
            copy.wait_recv()
        own, got = r.mine[...], r.theirs[...]
        sides = (jnp.where(core == 0, own, got), jnp.where(core == 0, got, own))
        for group in range(SIDE):
            side, n = sides[group // 2], group % 2
            pieces = [side[:, n * HEADS * HS : (n + 1) * HEADS * HS]]
            for kv in range(KVS):
                first = (n * KVS + kv) * HS
                pieces.append(side[:, nq + first : nq + first + HS])
                pieces.append(side[:, nq + nk + first : nq + nk + first + HS])
            r.blocks[group] = jnp.concatenate(pieces, axis=1)
        sends = [
            misc.to(at(place, 0, k), r.blocks.at[wrap(y + k)], r.w_heads.at[y, z, core])
            for k in (1, -1, 2)
        ]
        r.w_heads[y, z, core] = r.blocks[y]
        yield 0
        for copy in sends:
            copy.wait_recv()

        def pieces(pos, part):
            lead = pl.ds(0, SIDE) if part is None else pl.ds(part * 2, 2)
            return [r.w_heads.at[lead, pos, core]]

        yield from spread(RingGather(misc, along_z, pieces), pieces, z)

    def out_flow():
        for copy in kept_out:
            copy.wait()
        for copy in out_swaps:
            copy.wait_recv()
        yield from multicast(r.strips, r.w_out)

    def angle_flow():
        base = (core * SIDE + z) * QB
        index = base + lax.broadcasted_iota(jnp.int32, (QB, WIDE), 0)
        begin = jnp.zeros((QB, WIDE), jnp.int32)
        first = jnp.int32(0)
        for s in range(r.lengths.shape[1]):
            begin = jnp.where(index >= first, jnp.maximum(begin, first), begin)
            first = first + r.lengths[0, s]
        r.start[...] = begin[:, :1] - (base - LONGEST)
        lanes = lane((QB, WIDE))
        freqs = jnp.exp((lanes % (HS // 2)).astype(F32) * (-2.0 * 13.122363377404328 / HS))
        turned = (index - begin).astype(F32) * freqs
        r.cos[...] = jnp.cos(turned)
        sine = jnp.sin(turned)
        r.sin[...] = jnp.where(lanes % HS < HS // 2, -sine, sine)
        yield 0

    gather = Gather(place, r.cots, Slabs(r.cot.shape[0]), r.gs, r.gr, own=r.cot)

    def cot_flow():
        yield from gather.steps()
        kept_cot.wait()
        gather.finish()
        yield 6

    plan.add("a", feed_flow(0))
    plan.add("b", feed_flow(1))
    plan.add("c", feed_flow(2))
    plan.add("w", head_flow())
    plan.add("o", out_flow())
    plan.add("t", angle_flow())
    plan.add("k", cot_flow())
    plan.point()

    kept_x.wait()
    plan.point()
    for copy in x_moves:
        copy.wait_recv()
    x = r.xt[...].astype(F32)
    r.x_all[:, span(y, DEEP)] = (x * gain_row(r.gains, 0)).astype(BF16)

    def rows_of(ref):
        def pieces(pos, part):
            rows = pl.ds(0, QB) if part is None else pl.ds(part * (QB // 2), QB // 2)
            return [ref.at[rows, span(pos, DEEP)]]

        return pieces

    x_ring = RingGather(misc, along_y, rows_of(r.x_all))
    x_ring.start()
    r.stat[...] = row_sums(x * x)
    square = AxisTotals(place, r.stat, r.slots, r.ts, r.tr)
    plan.point()
    plan.point()
    x_ring.relay()
    plan.point()
    plan.point()
    x_ring.finish()
    rms = lax.rsqrt(jnp.transpose(square.finish())[:, :1] / width + EPS)
    r.rms[...] = rms
    plan.point()
    plan.drain("tw")
    plan.point()

    cosine, sine = r.cos[...], r.sin[...]
    halo = None
    for n in reversed(range(HEAD_WIDTH // QB)):
        weights = r.w_heads[..., n * QB : (n + 1) * QB].reshape(width, QB)
        raw = nn(r.x_all[...], weights) * rms
        r.raw[:, n * QB : (n + 1) * QB] = raw
        for m in range(2):
            piece = raw[:, m * WIDE : (m + 1) * WIDE]
            rotated = turn(piece, cosine, sine)
            at_head = n * 2 + m
            if at_head < HEADS // 2:
                r.q[:, at_head * WIDE : (at_head + 1) * WIDE] = rotated.astype(BF16)
            else:
                kv = jnp.where(lane(piece.shape) < HS, rotated, piece)
                r.kvs[at_head - HEADS // 2, LONGEST:, :] = kv.astype(BF16)
        if halo is None:
            halo = [
                misc.to(
                    tile_peer(place, k),
                    r.kvs.at[side, pl.ds(LONGEST, QB), :],
                    r.kvs.at[side, pl.ds(LONGEST - k * QB, QB), :],
                )
                for side in range(KVS)
                for k in (1, 2)
            ]
    plan.point()
    plan.point()
    for j in range(SIDE):
        if j % 2 == 0:
            for copy in halo[j : j + 2]:
                copy.wait_recv()
        plan.point()
        attend_pair(r, jnp.int32(j))
    plan.point()
    plan.drain("o")

    heads = r.heads[...]
    for n in range(SIDE):
        r.terms[:, pl.ds(n * DEEP, DEEP)] = nn(heads, out_weights(r, n)).astype(BF16)
    term_ring = RingScatter(
        misc,
        along_y,
        rows_of(r.terms),
        [[r.half_terms.at[n]] for n in range(2)],
        [[r.full_terms.at[n]] for n in range(2)],
    )
    term_ring.start()
    plan.point()
    term_ring.relay()
    plan.point()
    plan.point()
    term_ring.wait()
    r.hidden[...] = r.xt[...].astype(F32) + term_ring.total()
    for name in ("xt", "x_all", "heads", "hidden", "raw", "q", "kvs", "rms", "cos", "sin"):
        local.move(getattr(r, name), getattr(r, name + "_out"))
    for name in ("start", "gains", "w_heads", "w_out"):
        local.move(getattr(r, name), getattr(r, name + "_out"))
    return misc, deals, flows


def take(ref, chunk, columns=slice(None)):
    size = QB // 2
    pieces = [
        ref[n * QB + chunk * size : n * QB + (chunk + 1) * size, columns] for n in range(SIDE)
    ]
    return jnp.concatenate(pieces, axis=0)


def put(ref, chunk, values, columns=slice(None)):
    size = QB // 2
    for n in range(SIDE):
        rows = slice(n * QB + chunk * size, n * QB + (chunk + 1) * size)
        ref[rows, columns] = values[n * size : (n + 1) * size]


def feed_chunk(r, chunk):
    unit = r.act.shape[1] // 2
    rms = take(r.rms2, chunk)
    left = take(r.normed, chunk)
    dots = None
    for side in range(2):
        columns = slice(side * unit, (side + 1) * unit)
        both = nn(left, r.gu[side].reshape(COLS * WIDE, -1)) * rms
        gate, up = both[:, :unit], both[:, unit:]
        sigma = 1.0 / (1.0 + jnp.exp(-gate))
        swish = gate * sigma
        put(r.act, chunk, (swish * up).astype(BF16), columns)
        grad_act = take(r.grad_act, chunk, columns)
        grad_gate = grad_act * up * sigma * (1.0 + gate * (1.0 - sigma))
        grad_up = grad_act * swish
        term = grad_gate * gate + grad_up * up
        dots = term if side == 0 else dots + term
        grads = jnp.concatenate([grad_gate, grad_up], axis=1)
        columns = slice(2 * side * unit, 2 * (side + 1) * unit)
        put(r.grads, chunk, (grads * rms).astype(BF16), columns)
        r.plain[:, columns] = grads.astype(BF16)
        yield side
    for n in range(SIDE):
        columns = slice(n * DEEP, (n + 1) * DEEP)
        rows = pl.ds(n * SIDE, SIDE)
        part = nt(r.plain[:, : 2 * unit], r.gu[0, rows].reshape(DEEP, -1))
        part = part + nt(r.plain[:, 2 * unit :], r.gu[1, rows].reshape(DEEP, -1))
        put(r.part, chunk, part.astype(BF16), columns)
        if n % 2 == 1:
            yield 1 + n
    sums = row_sums(dots)
    size = QB // 2
    for n in range(SIDE):
        lanes = slice(n * QB + chunk * size, n * QB + (chunk + 1) * size)
        r.stat2[:, lanes] = sums[:, n * size : (n + 1) * size]


def middle(r, place, plan, local):
    z, y = place
    width = COLS * WIDE
    unit = r.act.shape[1] // 2
    down = lambda columns: r.d[:, :, :, columns].reshape(2 * unit, -1)
    chunk = QB // 2
    gain = gain_row(r.gains, 1)
    hidden = r.hidden[...]
    r.normed[span(z, QB), span(y, DEEP)] = (hidden * gain).astype(BF16)
    gathers = [
        Gather(place, r.normed, Tiles(n * chunk, chunk), send, recv)
        for n, (send, recv) in enumerate(((r.gs0, r.gr0), (r.gs1, r.gr1)))
    ]

    def pull_flow():
        for i in range(2):
            here = pl.ds(2 * i * QB, 2 * QB)
            r.grad_act[here, :] = nt(r.cots[here, :], down(slice(None)))
            yield i

    plan.add("1", gathers[0].steps())
    plan.add("2", gathers[1].steps())
    plan.point()
    r.stat1[...] = row_sums(hidden * hidden)
    square = AxisTotals(place, r.stat1, r.slots1, r.ts1, r.tr1)
    plan.point()
    own = r.stats.at[:, span(z, QB)]
    own[...] = square.finish()
    shares = Copies(r.zs, r.zr)
    for k in (1, -1, 2):
        shares.to(at(place, k, 0), own, own)
    plan.point()
    plan.point()
    plan.point()
    plan.point()
    for copy in shares.open:
        copy.wait_recv()
    r.rms2[...] = lax.rsqrt(jnp.transpose(r.stats[...])[:, :1] / width + EPS)
    plan.drain("ck")
    local.move(r.d, r.d_out)
    plan.add("p", pull_flow())
    plan.point()
    plan.drain("p1ab")
    gathers[0].finish()
    for n in feed_chunk(r, 0):
        if n != 1:
            plan.point()
    scatters = [
        Scatter(place, r.part, Tiles(n * chunk, chunk), halves, quarters, send, recv)
        for n, (halves, quarters, send, recv) in enumerate(
            (
                (r.halves0, r.quarters0, r.ss0, r.sr0),
                (r.halves1, r.quarters1, r.ss1, r.sr1),
            )
        )
    ]
    plan.add("3", scatters[0].steps())
    plan.point()
    plan.drain("2")
    gathers[1].finish()
    for n in feed_chunk(r, 1):
        if n == SIDE:
            plan.add("4", scatters[1].steps())
        plan.point()
    sums = Totals(place, r.stat2, r.mid2, r.slots2, r.ts2, r.tr2)
    sums.first()


    def both_flow():
        for b in range(SIDE):
            four = tn(r.normed[:, pl.ds(b * DEEP, DEEP)], r.grads[...])
            here = pl.ds(SIDE * b, SIDE)
            r.gu_sum[here] = four.astype(BF16).reshape(SIDE, *r.gu_sum.shape[1:])
            local.move(r.gu_sum.at[here], r.gu_grad.at[here])
            yield b

    def down_flow():
        for n in range(SIDE):
            columns = pl.ds(n * DEEP, DEEP)
            block = tn(r.act[...], r.cots[:, columns])
            r.d_sum[:, :, :, columns] = block.astype(BF16).reshape(*r.d_sum.shape[:3], DEEP)
            if n == SIDE - 1:
                local.move(r.d_sum, r.d_grad)
            yield n

    plan.add("e", both_flow())
    plan.add("f", down_flow())
    local.move(r.act, r.act_out)
    plan.point()
    plan.point()
    sums.second()
    plan.point()
    plan.point()
    plan.drain("3ef4")
    r.stat2[...] = sums.finish()
    mean = jnp.transpose(r.stat2[:, span(z, QB)])[:, :1] / width
    gain_sum = jnp.zeros((1, DEEP), F32)
    for scatter in scatters:
        for (first, size), summed in scatter.results:
            here = pl.ds(first, size)
            there = pl.ds(pl.multiple_of(z * QB + first, size), size)
            rms = r.rms2[there, :]
            xhat = r.hidden[here, :] * rms
            gain_sum = gain_sum + jnp.sum(summed * xhat, axis=0, keepdims=True)
            r.grad[here, :] = r.cots[there, span(y, DEEP)].astype(F32) + rms * (
                gain * summed - xhat * mean[first : first + size]
            )
    r.gain_two_out[...] = gain_sum
    shares.finish()
    for scatter in scatters:
        scatter.finish()


def ahead(r):
    place = spot()
    plan = Plan(AHEAD_PLAN)
    local = Locals(r.local)
    groups = front(r, place, plan, local)
    kept = len(local.open) - 14
    middle(r, place, plan, local)
    for copy in local.open[kept:]:
        copy.wait()
    for group in groups:
        group.finish()


def call_ahead(x, gain_one, gain_two, cot, wq, wk, wv, wo, wg, wu, wd, lengths):
    rows, depth = x.shape
    wide = COLS * depth
    unit = wd.shape[0] // COLS
    share, tall = depth // SIDE, unit // SIDE
    strip = wo.shape[0] // 16
    inputs = dict(x=x, gain_one=gain_one, gain_two=gain_two, cot=cot, wq=wq, wk=wk, wv=wv)
    inputs.update(wo=wo, wg=wg, wu=wu, wd=wd, lengths=lengths)
    inputs = {name: (array, ANY) for name, array in inputs.items()}
    inputs["gain_one"] = (gain_one, VMEM)
    inputs["gain_two"] = (gain_two, VMEM)
    inputs["lengths"] = (lengths, SMEM)
    kept = dict(
        xt=shape((QB, DEEP)),
        x_all=shape((QB, wide)),
        heads=shape((QB, HEADS * HS)),
        hidden=shape((QB, DEEP), F32),
        raw=shape((QB, HEAD_WIDTH), F32),
        q=shape((QB, HEADS * HS)),
        kvs=shape((KVS, WIN, 2 * HS)),
        rms=shape((QB, 1), F32),
        cos=shape((QB, WIDE), F32),
        sin=shape((QB, WIDE), F32),
        start=shape((QB, 1), jnp.int32),
        gains=shape((SIDE, 8, WIDE), F32),
        w_heads=shape((SIDE, SIDE, 2, depth // 2, HEAD_WIDTH)),
        w_out=shape((SIDE, SIDE, SIDE, 2, strip, depth)),
    )
    gu_shape = (COLS, SIDE, share, 4 * unit)
    d_shape = (2, SIDE, tall, wide)
    outs = {name + "_out": (value, ANY) for name, value in kept.items()}
    outs.update(
        grad=(shape((QB, DEEP), F32), VMEM),
        gain_two_out=(shape((1, DEEP), F32), VMEM),
        act_out=(shape((rows, 2 * unit)), ANY),
        d_out=(shape(d_shape), ANY),
        gu_grad=(shape(gu_shape), ANY),
        d_grad=(shape(d_shape), ANY),
    )
    scratch = {name: pltpu.VMEM(value.shape, value.dtype) for name, value in kept.items()}
    scratch.update(
        mine=pltpu.VMEM((depth // 2, wq.shape[1] + 2 * wk.shape[1]), BF16),
        theirs=pltpu.VMEM((depth // 2, wq.shape[1] + 2 * wk.shape[1]), BF16),
        blocks=pltpu.VMEM((SIDE, depth // 2, HEAD_WIDTH), BF16),
        strips=pltpu.VMEM((SIDE, strip, depth), BF16),
        terms=pltpu.VMEM((QB, wide), BF16),
        half_terms=pltpu.VMEM((2, QB // 2, DEEP), BF16),
        full_terms=pltpu.VMEM((2, QB, DEEP), BF16),
        stat=pltpu.VMEM((8, QB), F32),
        slots=pltpu.VMEM((3, 8, QB), F32),
        stat1=pltpu.VMEM((8, QB), F32),
        slots1=pltpu.VMEM((3, 8, QB), F32),
        normed=pltpu.VMEM((rows, wide), BF16),
        gu=pltpu.VMEM((2, COLS, SIDE, share, 2 * unit), BF16),
        d=pltpu.VMEM(d_shape, BF16),
        cots=pltpu.VMEM((rows, wide), BF16),
        part=pltpu.VMEM((rows, wide), BF16),
        act=pltpu.VMEM((rows, 2 * unit), BF16),
        grads=pltpu.VMEM((rows, 4 * unit), BF16),
        grad_act=pltpu.VMEM((rows, 2 * unit), F32),
        plain=pltpu.VMEM((rows // 2, 4 * unit), BF16),
        gu_sum=pltpu.VMEM(gu_shape, BF16),
        d_sum=pltpu.VMEM(d_shape, BF16),
        rms2=pltpu.VMEM((rows, 1), F32),
        halves0=pltpu.VMEM((20, QB // 4, DEEP), BF16),
        quarters0=pltpu.VMEM((20, QB // 8, DEEP), BF16),
        halves1=pltpu.VMEM((20, QB // 4, DEEP), BF16),
        quarters1=pltpu.VMEM((20, QB // 8, DEEP), BF16),
        stats=pltpu.VMEM((8, rows), F32),
        stat2=pltpu.VMEM((8, rows), F32),
        mid2=pltpu.VMEM((8, rows), F32),
        slots2=pltpu.VMEM((6, 8, rows), F32),
    )
    for name, size in (("t", 3), ("g", Gather.COUNT), ("m", 72), ("b", 3 * (COLS - 1)), ("w", 12)):
        scratch[name + "s"] = dma(size)
        scratch[name + "r"] = dma(size)
    for name, size in (("1", 3), ("2", 6)):
        scratch["ts" + name] = dma(size)
        scratch["tr" + name] = dma(size)
    scratch["zs"] = dma(3)
    scratch["zr"] = dma(3)
    for name in ("gs0", "gr0", "gs1", "gr1", "ss0", "sr0", "ss1", "sr1"):
        scratch[name] = dma(Gather.COUNT)
    scratch["local"] = dma(48)
    return launch(ahead, 1, inputs, outs, scratch)


class FeedSum:
    def __init__(self, r, name):
        self.r, self.name = r, name
        self.core, self.me = lax.axis_index("row"), lax.axis_index("col")
        self.quarter = lax.axis_index("dp")
        for part in ("sum", "came", "half", "full"):
            setattr(self, part, getattr(r, f"{name}_{part}"))
        self.out = getattr(r, f"{name}_out")
        self.copies = Copies(getattr(r, f"{name}_send"), getattr(r, f"{name}_recv"))

    def _grad(self, core):
        r = self.r
        if self.name == "down":
            return r.d_grad.at[core]
        unit = self.sum.shape[3]
        first = core * 2 * unit + (unit if self.name == "up" else 0)
        return r.gu_grad.at[:, :, :, pl.ds(pl.multiple_of(first, unit), unit)]

    def _pieces(self, pos, part):
        if self.name == "down":
            tall = self.sum.shape[1]
            rows = pl.ds(0, tall) if part is None else pl.ds(part * (tall // 2), tall // 2)
            return [self.sum.at[pos, rows, :]]
        chips = pl.ds(0, COLS) if part is None else pl.ds(part * (COLS // 2), COLS // 2)
        return [self.sum.at[chips, pos]]

    def _outs(self, pos, part):
        if self.name == "down":
            chips = pl.ds(0, COLS) if part is None else pl.ds(part * (COLS // 2), COLS // 2)
            return [self.out.at[chips, pos]]
        size = self.out.shape[1]
        cut = pl.ds(0, size) if part is None else pl.ds(part * (size // 2), size // 2)
        return [self.out.at[span(pos, self.sum.shape[2]), cut]]

    def steps(self):
        g = self.quarter
        load = self.r.locals.move(self._grad(self.core), self.sum)
        swap = self.copies.to(other_core(), self._grad(1 - self.core), self.came)
        yield 0
        load.wait()
        swap.wait_recv()

        def add(i, carry):
            self.sum[i] = self.sum[i] + self.came[i]
            return carry

        lax.fori_loop(0, self.sum.shape[0], add, 0)
        ring = RingScatter(
            self.copies,
            Along("dp"),
            self._pieces,
            [[self.half.at[n]] for n in range(2)],
            [[self.full.at[n]] for n in range(2)],
        )
        ring.start()
        yield 1
        ring.relay()
        yield 2
        ring.wait()
        (mine,) = self._pieces(g, None)
        mine[...] = ring.total().astype(BF16)
        deals = []
        for k in range(COLS):
            c = chip(k)
            where = lax.rem(c, SIDE) * SIDE + lax.div(c, SIDE)
            if self.name == "down":
                source, target = mine.at[:, span(where, WIDE)], self.out.at[self.me, g]
            else:
                source = self.sum.at[where, g]
                target = self.out.at[span(g, self.sum.shape[2]), span(self.me, self.sum.shape[3])]
            if k == 0:
                deals.append(self.r.locals.move(source, target).wait)
            else:
                deals.append(self.copies.to({"col": c}, source, target).wait_recv)
        yield 3
        for wait in deals:
            wait()
        ring = RingGather(self.copies, Along("dp"), self._outs)
        ring.start()
        yield 4
        ring.relay()
        yield 5
        ring.finish()
        yield 6


class GroupSum:
    def __init__(self, r, place, name):
        self.place = place
        for part in ("grad", "sum", "half", "full", "part", "came", "own", "dealt", "out"):
            setattr(self, part, getattr(r, f"{name}_{part}"))
        self.copies = Copies(getattr(r, f"{name}_send"), getattr(r, f"{name}_recv"))

    def steps(self):
        z, y = place = self.place
        core, g = lax.axis_index("row"), lax.axis_index("dp")
        to = self.copies.to
        swap = to(other_core(), self.grad.at[:, :, 1 - core], self.sum)
        yield 0
        swap.wait_recv()

        def add(i, carry):
            self.sum[i] = self.sum[i] + self.grad[i, :, core]
            return carry

        lax.fori_loop(0, SIDE, add, 0)

        def pieces(pos, part):
            lead = pl.ds(0, SIDE) if part is None else pl.ds(part * 2, 2)
            return [self.sum.at[lead, pos]]

        ring = RingScatter(
            self.copies,
            Along("z", place),
            pieces,
            [[self.half.at[n]] for n in range(2)],
            [[self.full.at[n]] for n in range(2)],
        )
        ring.start()
        yield 1
        ring.relay()
        yield 2
        ring.wait()
        total = ring.total().astype(BF16)
        size = self.part.shape[2]
        for k in range(SIDE):
            self.part[k] = total[:, k * size : (k + 1) * size]
        sends = [
            to(beside(k), self.part.at[wrap(g + k)], self.came.at[i])
            for i, k in enumerate((1, -1, 2))
        ]
        yield 3
        for copy in sends:
            copy.wait_recv()
        there = (self.came[0].astype(F32) + self.came[1].astype(F32)) + self.came[2].astype(F32)
        self.own[...] = (self.part[g].astype(F32) + there).astype(BF16)
        deals = [
            to(at(place, 0, k), self.own.at[wrap(y + k)], self.dealt.at[y]) for k in (1, -1, 2)
        ]
        self.dealt[y] = self.own[y]
        yield 4
        for copy in deals:
            copy.wait_recv()
        cross = to(other_core(), self.dealt.at[pl.ds(2 * (1 - core), 2)], self.out.at[:, core, g])
        self.out[:, core, g] = self.dealt[pl.ds(2 * core, 2)]
        yield 5
        cross.wait_recv()
        mine = self.out.at[:, :, g]
        rounds = [to(beside(k), mine, mine) for k in range(1, SIDE)]
        yield 6
        for copy in rounds:
            copy.wait_recv()
        yield 7


BACK_PLAN = (
    "gd",
    "gp",
    "d",
    "upg",
    "up",
    "",
    "d",
    "g",
    "u",
    "h",
    "doghuod",
    "h",
    "i",
    "u",
    "ido",
    "iph",
    "oh",
    "nip",
    "ghuoinp",
    "hpdo",
    "gpinuopip",
)


def back(r):
    place = z, y = spot()
    g = lax.axis_index("dp")
    width = COLS * WIDE
    plan = Plan(BACK_PLAN)
    count = hail(place, wide=True)
    r.locals = Locals(r.local)
    in_act = r.locals.move(r.act_in, r.act)
    in_down = r.locals.move(r.down_in, r.down)
    in_out = r.locals.move(r.w_out_in, r.w_out)
    r.lows[:, span(y, DEEP)] = r.grad[...].astype(BF16)
    r.dkv[...] = jnp.zeros_like(r.dkv)
    meet(count)
    misc, small = Copies(r.ms, r.mr), Copies(r.ns, r.nr)
    along_y = Along("y", place)

    def cut(ref):
        def pieces(pos, part):
            rows = pl.ds(0, QB) if part is None else pl.ds(part * (QB // 2), QB // 2)
            return [ref.at[rows, span(pos, DEEP)]]

        return pieces

    low_ring = RingGather(misc, along_y, cut(r.lows))
    low_ring.start()
    feeds = [FeedSum(r, name) for name in ("gate", "up", "down")]
    scatter = Scatter(place, r.out_sum, Slabs(r.out_sum.shape[0]), r.halves, r.quarters, r.ss, r.sr)

    def output_flow():
        in_act.wait()
        in_down.wait()
        for i in range(SIDE):
            here = pl.ds(i * QB, QB)
            left = r.act[here, :]
            for n in range(SIDE):
                columns = pl.ds(n * DEEP, DEEP)
                weights = r.down[:, :, :, columns].reshape(left.shape[1], DEEP)
                r.out_sum[here, columns] = nn(left, weights).astype(BF16)
            if i == 1:
                yield -1
        own = r.out_sum.at[span(z, QB), span(y, DEEP)]
        own[...] = (own[...].astype(F32) + r.hidden[...]).astype(BF16)
        yield from scatter.steps()
        for (first, rows), value in scatter.results:
            r.output[pl.ds(first, rows), :] = value.astype(BF16)
        yield 9

    for letter, feed in zip("gud", feeds, strict=True):
        plan.add(letter, feed.steps())
    plan.add("p", output_flow())
    plan.point()
    in_heads = r.locals.move(r.w_heads_in, r.w_heads)
    in_x = r.locals.move(r.x_all_in, r.x_all)
    in_raw = r.locals.move(r.raw_in, r.raw)
    plan.point()
    low_ring.relay()
    plan.point()
    plan.point()
    in_out.wait()
    low_ring.finish()

    grad = None
    for n in range(SIDE):
        term = nt(r.lows[:, n * DEEP : (n + 1) * DEEP], out_weights(r, n))
        grad = term if n == 0 else grad + term
    r.gheads[...] = grad.astype(BF16)
    plan.point()

    halo = []
    for j in range(SIDE):
        attend_pair_back(r, jnp.int32(j))
        if j % 2 == 1:
            side = j // 2
            for n in range(2):
                r.halo[n, side] = r.dkv[side, n * QB : (n + 1) * QB].astype(BF16)
                peer = tile_peer(place, n - 2)
                halo.append(misc.to(peer, r.halo.at[n, side], r.halo.at[2 + n, side]))
        plan.point()

    cosine, sine = r.cos[...], -r.sin[...]
    grad_q = jnp.concatenate(
        [turn(r.dq[:, n * WIDE : (n + 1) * WIDE], cosine, sine) for n in range(HEADS // 2)],
        axis=1,
    )
    in_x.wait()
    rms = r.rms[...]

    def weight_grads(target, grads):
        grads = (grads * rms).astype(BF16)
        for n in range(SIDE):
            block = tn(r.x_all[:, n * DEEP : (n + 1) * DEEP], grads).astype(BF16)
            target[n] = block.reshape(*target.shape[1:])

    weight_grads(r.q_grad, grad_q)
    queries = GroupSum(r, place, "q")
    plan.add("h", queries.steps())
    plan.point()

    turned_heads = jnp.transpose(r.heads[...].astype(F32)).astype(BF16)
    for n in range(SIDE):
        block = nn(turned_heads, r.lows[:, n * DEEP : (n + 1) * DEEP]).astype(BF16)
        for k in range(SIDE):
            columns = slice(k * WIDE, (k + 1) * WIDE)
            r.o_grad[n, k] = block[:, columns].reshape(*r.o_grad.shape[2:])
    outs = GroupSum(r, place, "o")
    plan.add("o", outs.steps())
    plan.point()
    plan.point()
    for copy in halo:
        copy.wait_recv()
    in_heads.wait()
    in_raw.wait()
    pieces = []
    for n in range(KVS):
        kv = r.dkv[n, LONGEST:] + (r.halo[2, n].astype(F32) + r.halo[3, n].astype(F32))
        pieces.append(jnp.where(lane(kv.shape) < HS, turn(kv, cosine, sine), kv))
    grad_kv = jnp.concatenate(pieces, axis=1)
    low_q, low_kv = grad_q.astype(BF16), grad_kv.astype(BF16)
    for n in range(SIDE):
        weights = r.w_heads[n].reshape(DEEP, HEAD_WIDTH)
        term = nt(low_q, weights[:, : HEADS * HS]) + nt(low_kv, weights[:, HEADS * HS :])
        r.terms[:, pl.ds(n * DEEP, DEEP)] = term.astype(BF16)
    term_ring = RingScatter(
        misc,
        along_y,
        cut(r.terms),
        [[r.half_terms.at[n]] for n in range(2)],
        [[r.full_terms.at[n]] for n in range(2)],
    )
    term_ring.start()

    weight_grads(r.k_grad, grad_kv)
    keys = GroupSum(r, place, "k")
    plan.add("i", keys.steps())
    plan.point()
    whole = jnp.concatenate([grad_q, grad_kv], axis=1)
    r.stat[...] = row_sums(whole * r.raw[...])
    dots = AxisTotals(place, r.stat, r.slots, r.ts, r.tr)
    plan.point()
    term_ring.relay()
    plan.point()
    plan.point()
    term_ring.wait()
    mean = jnp.transpose(dots.finish())[:, :1] / width
    xhat = r.xt[...].astype(F32) * rms
    summed = term_ring.total()
    gain_sum = jnp.sum(summed * xhat, axis=0, keepdims=True)
    result = r.grad[...] + rms * (gain_row(r.gains, 0) * summed - xhat * mean)
    for k in range(SIDE):
        r.result[k] = result[:, k * WIDE : (k + 1) * WIDE].astype(BF16)
    landing = r.grad_input.at[span(z, QB), :]
    sends = [
        misc.to(at(place, k, 0), r.result.at[wrap(z + k)], landing) for k in (1, -1, 2)
    ]
    landing[...] = r.result[z]

    def gain_flow():
        row = lax.broadcasted_iota(jnp.int32, (8, WIDE), 0)
        gain_two = r.gain_two[...]
        for k in range(SIDE):
            lanes = slice(k * WIDE, (k + 1) * WIDE)
            r.gain_part[k] = jnp.where(row == 0, gain_sum[:, lanes], gain_two[:, lanes])
        moves = [
            small.to(at(place, k, 0), r.gain_part.at[wrap(z + k)], r.gain_z.at[z])
            for k in (1, -1, 2)
        ]
        r.gain_z[z] = r.gain_part[z]
        yield 0
        for copy in moves:
            copy.wait_recv()
        r.gain_mine[...] = (r.gain_z[0] + r.gain_z[1]) + (r.gain_z[2] + r.gain_z[3])
        crossing = small.to(other_core(), r.gain_mine, r.gain_core)
        yield 1
        crossing.wait_recv()
        mine = r.gain_dp.at[g]
        mine[...] = r.gain_core[...] + r.gain_mine[...]
        moves = [small.to(beside(k), mine, mine) for k in range(1, SIDE)]
        yield 2
        for copy in moves:
            copy.wait_recv()
        r.gain_out[...] = (r.gain_dp[0] + r.gain_dp[1]) + (r.gain_dp[2] + r.gain_dp[3])
        yield 3

    plan.add("n", gain_flow())
    for _ in range(5):
        plan.point()
    plan.drain("nohigudp")
    for copy in sends:
        copy.wait_recv()
    scatter.finish()
    for group in (misc, small, queries.copies, keys.copies, outs.copies, *(feed.copies for feed in feeds)):
        group.finish()


def call_back(f):
    rows, wide = f.act_out.shape[0], COLS * WIDE
    share, tall, unit = f.gu_grad.shape[2], f.d_grad.shape[2], f.gu_grad.shape[3] // 4
    strip, half, depth = 4 * f.w_out_out.shape[4], f.w_heads_out.shape[3], WIDE
    inputs = {
        name: (getattr(f, name + "_out"), VMEM)
        for name in ("xt", "heads", "hidden", "q", "kvs", "rms", "cos", "sin", "start", "gains")
    }
    inputs.update(grad=(f.grad, VMEM), gain_two=(f.gain_two_out, VMEM), act_in=(f.act_out, ANY), down_in=(f.d_out, ANY))
    inputs.update(gu_grad=(f.gu_grad, ANY), d_grad=(f.d_grad, ANY))
    for name in ("x_all", "raw", "w_heads", "w_out"):
        inputs[name + "_in"] = (getattr(f, name + "_out"), ANY)
    outs = dict(
        output=(shape((rows, WIDE)), VMEM),
        grad_input=(shape((rows, WIDE)), VMEM),
        gain_out=(shape((8, WIDE), F32), VMEM),
        gate_out=(shape((WIDE, COLS * unit)), ANY),
        up_out=(shape((WIDE, COLS * unit)), ANY),
        down_out=(shape((COLS, SIDE, tall, WIDE)), ANY),
        o_out=(shape((2, 2, SIDE, strip // SIDE, WIDE)), VMEM),
        q_out=(shape((2, 2, SIDE, half // SIDE, HEADS * HS)), VMEM),
        k_out=(shape((2, 2, SIDE, half // SIDE, 2 * KVS * HS)), VMEM),
    )
    scratch = {
        name: pltpu.VMEM(getattr(f, name + "_out").shape, getattr(f, name + "_out").dtype)
        for name in ("x_all", "raw", "w_heads", "w_out")
    }
    scratch.update(
        out_sum=pltpu.VMEM((rows, wide), BF16),
        act=pltpu.VMEM(f.act_out.shape, BF16),
        down=pltpu.VMEM(f.d_out.shape, BF16),
        halves=pltpu.VMEM((20, rows // 2, WIDE), BF16),
        quarters=pltpu.VMEM((20, rows // 4, WIDE), BF16),
        lows=pltpu.VMEM((QB, wide), BF16),
        gheads=pltpu.VMEM((QB, HEADS * HS), BF16),
        dq=pltpu.VMEM((QB, HEADS * HS), F32),
        dkv=pltpu.VMEM((KVS, WIN, 2 * HS), F32),
        halo=pltpu.VMEM((4, KVS, QB, 2 * HS), BF16),
        terms=pltpu.VMEM((QB, wide), BF16),
        half_terms=pltpu.VMEM((2, QB // 2, DEEP), BF16),
        full_terms=pltpu.VMEM((2, QB, DEEP), BF16),
        result=pltpu.VMEM((SIDE, QB, WIDE), BF16),
        stat=pltpu.VMEM((8, QB), F32),
        slots=pltpu.VMEM((3, 8, QB), F32),
        ts=dma(3),
        tr=dma(3),
        ss=dma(Scatter.COUNT),
        sr=dma(Scatter.COUNT),
    )
    for name, lead, piece in (
        ("gate", (COLS,), (share, unit)),
        ("up", (COLS,), (share, unit)),
        ("down", (), (tall, wide)),
    ):
        whole = lead + (SIDE,) + piece
        first = lead[0] // 2 if lead else tall // 2
        scratch[name + "_sum"] = pltpu.VMEM(whole, BF16)
        scratch[name + "_came"] = pltpu.VMEM(whole, BF16)
        halves = (first,) + (piece if lead else piece[1:])
        scratch[name + "_half"] = pltpu.VMEM((2,) + halves, BF16)
        scratch[name + "_full"] = pltpu.VMEM((2,) + lead + piece, BF16)
        scratch[name + "_send"] = dma(COLS + 10)
        scratch[name + "_recv"] = dma(COLS + 10)
    for name, piece in (
        ("q", (half, HEADS * HS)),
        ("k", (half, 2 * KVS * HS)),
        ("o", (strip, depth)),
    ):
        small = (SIDE, piece[0] // SIDE, piece[1])
        scratch[name + "_grad"] = pltpu.VMEM((SIDE, SIDE, 2) + piece, BF16)
        scratch[name + "_sum"] = pltpu.VMEM((SIDE, SIDE) + piece, BF16)
        scratch[name + "_half"] = pltpu.VMEM((2, 2) + piece, BF16)
        scratch[name + "_full"] = pltpu.VMEM((2, SIDE) + piece, BF16)
        scratch[name + "_part"] = pltpu.VMEM((SIDE,) + small, BF16)
        scratch[name + "_came"] = pltpu.VMEM((3,) + small, BF16)
        scratch[name + "_own"] = pltpu.VMEM(small, BF16)
        scratch[name + "_dealt"] = pltpu.VMEM(small, BF16)
        scratch[name + "_send"] = dma(16)
        scratch[name + "_recv"] = dma(16)
    scratch.update(
        gain_part=pltpu.VMEM((SIDE, 8, WIDE), F32),
        gain_z=pltpu.VMEM((SIDE, 8, WIDE), F32),
        gain_mine=pltpu.VMEM((8, WIDE), F32),
        gain_core=pltpu.VMEM((8, WIDE), F32),
        gain_dp=pltpu.VMEM((SIDE, 8, WIDE), F32),
        ns=dma(8),
        nr=dma(8),
        ms=dma(16),
        mr=dma(16),
        local=dma(12),
    )
    return launch(back, 2, inputs, outs, scratch)


def finish(gate, up, down, out, queries, pairs, total, grad, gains, *outs):
    gate_o, up_o, down_o, out_o, q_o, k_o, v_o, total_o, grad_o, one_o, two_o = outs
    gate_o[...] = gate[...].astype(F32)
    up_o[...] = up[...].astype(F32)
    down_o[...] = down[...].astype(F32)
    out_o[...] = out[...].astype(F32)
    keys, values = [], []
    for n in range(2):
        q_o[:, n * HEADS * HS : (n + 1) * HEADS * HS] = queries[n].astype(F32)
        whole = pairs[n].astype(F32)
        for kv in range(KVS):
            first = 2 * kv * HS
            keys.append(whole[:, first : first + HS])
            values.append(whole[:, first + HS : first + 2 * HS])
    k_o[...] = jnp.concatenate(keys, axis=1)
    v_o[...] = jnp.concatenate(values, axis=1)
    total_o[...] = total[...]
    grad_o[...] = grad[...].astype(F32)
    one_o[...] = gains[0:1, :]
    two_o[...] = gains[1:2, :]


def call_finish(b):
    arrays = (
        b.gate_out,
        b.up_out,
        b.down_out.reshape(-1, WIDE),
        b.o_out.reshape(-1, WIDE),
        b.q_out.reshape(2, WIDE, HEADS * HS),
        b.k_out.reshape(2, WIDE, 2 * KVS * HS),
        b.output,
        b.grad_input,
    )
    gate, up, down, out, queries, pairs, total, grad = arrays

    def cut(array):
        rows, columns = array.shape[-2] // 2, array.shape[-1]
        if len(array.shape) == 3:
            return pl.BlockSpec((array.shape[0], rows, columns), lambda i: (0, i, 0))
        return pl.BlockSpec((rows, columns), lambda i: (i, 0))

    small = pl.BlockSpec((1, WIDE), lambda i: (0, 0))
    outs = (
        shape(gate.shape, F32),
        shape(up.shape, F32),
        shape(down.shape, F32),
        shape(out.shape, F32),
        shape((WIDE, 2 * HEADS * HS), F32),
        shape((WIDE, 2 * KVS * HS), F32),
        shape((WIDE, 2 * KVS * HS), F32),
        shape(total.shape),
        shape(grad.shape, F32),
    )
    return pl.pallas_call(
        finish,
        grid=(2,),
        out_shape=outs + (shape((1, WIDE), F32),) * 2,
        in_specs=[cut(a) for a in arrays] + [pl.BlockSpec((8, WIDE), lambda i: (0, 0))],
        out_specs=tuple(cut(a) for a in outs) + (small, small),
        compiler_params=pltpu.CompilerParams(vmem_limit_bytes=60 * MIB),
        name="finish",
    )(*arrays, b.gain_out)


def on_device(
    block_input,
    gain_attn,
    w_query,
    w_key,
    w_value,
    w_out,
    gain_mlp,
    w_gate,
    w_up,
    w_down,
    lengths,
    cotangent,
):
    f = call_ahead(
        block_input,
        gain_attn,
        gain_mlp,
        cotangent,
        w_query,
        w_key,
        w_value,
        w_out,
        w_gate,
        w_up,
        w_down,
        lengths,
    )
    b = call_back(f)
    gate, up, down, out, query, key, value, output, grad_input, one, two = call_finish(b)
    return (
        output,
        grad_input,
        one.reshape(WIDE),
        query,
        key,
        value,
        out,
        two.reshape(WIDE),
        gate,
        up,
        down,
    )


def solution(mesh):
    in_specs = (
        P(("dp", "row"), "col"),
        P("col"),
        P("col", "row"),
        P("col", "row"),
        P("col", "row"),
        P("row", "col"),
        P("col"),
        P("col", "row"),
        P("col", "row"),
        P("row", "col"),
        P("dp", None),
        P(("dp", "row"), "col"),
    )
    out_specs = (
        P(("dp", "row"), "col"),
        P(("dp", "row"), "col"),
        P("col"),
        P("col", "row"),
        P("col", "row"),
        P("col", "row"),
        P("row", "col"),
        P("col"),
        P("col", "row"),
        P("col", "row"),
        P("row", "col"),
    )
    return jax.shard_map(
        on_device, mesh=mesh, in_specs=in_specs, out_specs=out_specs, check_vma=False
    )
```

```python
import types

import jax
import jax.numpy as jnp
from jax import lax
from jax.experimental import pallas as pl
from jax.experimental.pallas import tpu as pltpu
from jax.sharding import PartitionSpec as P

HQ = 32
HK = 8
HS = 64
LONGEST = 512
EPS = 1e-05
THETA = 500000.0
MESH = pl.DeviceIdType.MESH
SIDE = 4
COLS = SIDE * SIDE
WIDE = 128
DEEP = SIDE * WIDE
QB = 256
WIN = QB + LONGEST
HEADS = HQ // SIDE
KVS = HK // SIDE
HEAD_WIDTH = (HEADS + 2 * KVS) * HS
MIB = 1024 * 1024
BF16, F32 = jnp.bfloat16, jnp.float32


def spot():
    me = lax.axis_index("col")
    return lax.div(me, SIDE), lax.rem(me, SIDE)


def wrap(value):
    return lax.rem(value + SIDE, SIDE)


def off(place, offset):
    return wrap(place[0] + offset[0]), wrap(place[1] + offset[1])


def at(place, dz, dy):
    z, y = off(place, (dz, dy))
    return {"col": z * SIDE + y}


def shift(axis, amount):
    return (amount, 0) if axis == "z" else (0, amount)


def plus(one, two):
    return one[0] + two[0], one[1] + two[1]


def other_core():
    return {"row": 1 - lax.axis_index("row")}


def beside(step):
    return {"dp": wrap(lax.axis_index("dp") + step)}


def chip(step):
    return lax.rem(lax.axis_index("col") + step + COLS, COLS)


def tile_peer(place, step):
    tile = lax.rem(lax.axis_index("row") * SIDE + place[0] + step + 2 * SIDE, 2 * SIDE)
    return {"col": lax.rem(tile, SIDE) * SIDE + place[1], "row": lax.div(tile, SIDE)}


def hail(place, wide=False, far=False):
    barrier = pltpu.get_barrier_semaphore()
    if wide:
        peers = [{"col": chip(k)} for k in range(1, COLS)]
        peers += [beside(k) for k in range(1, SIDE)] + [other_core()]
        peers += [tile_peer(place, k) for k in (1, 2, -1, -2)]
        if far:
            peers += [{**beside(k), **other_core()} for k in range(1, SIDE)]
    else:
        peers = [at(place, *shift(axis, step)) for axis in ("z", "y") for step in (1, -1, 2)]
    for peer in peers:
        pl.semaphore_signal(barrier, inc=1, device_id=peer, device_id_type=MESH)
    return len(peers)


def meet(count):
    pl.semaphore_wait(pltpu.get_barrier_semaphore(), count)


def span(block, size):
    return pl.ds(pl.multiple_of(block * size, size), size)


class Plan:
    def __init__(self, words):
        self.words = list(words)
        self.flows = {}

    def add(self, letter, flow):
        self.flows[letter] = flow

    def step(self, letter):
        next(self.flows[letter], None)

    def point(self):
        if self.words:
            for letter in self.words.pop(0):
                self.step(letter)

    def drain(self, letters):
        for letter in letters:
            for _ in self.flows[letter]:
                pass


class Copies:
    def __init__(self, send, recv):
        self.send, self.recv, self.count = send, recv, 0
        self.open = []

    def to(self, peer, source, target):
        copy = pltpu.make_async_remote_copy(
            src_ref=source,
            dst_ref=target,
            send_sem=self.send.at[self.count],
            recv_sem=self.recv.at[self.count],
            device_id=peer,
            device_id_type=MESH,
        )
        self.count += 1
        copy.start()
        self.open.append(copy)
        return copy

    def finish(self):
        for copy in self.open:
            copy.wait_send()


class Locals:
    def __init__(self, sems):
        self.sems, self.open = sems, []

    def move(self, source, target):
        copy = pltpu.make_async_copy(source, target, self.sems.at[len(self.open)])
        copy.start()
        self.open.append(copy)
        return copy


class Slabs:
    def __init__(self, rows):
        self.rows = rows

    def lines(self, half, piece):
        size = self.rows // 2
        if piece is None:
            return half * size, size
        return half * size + piece * (size // 2), size // 2

    def part(self, ref, spot_of, half, piece):
        z, y = spot_of
        return ref.at[pl.ds(*self.lines(half, piece)), span(y * SIDE + z, WIDE)]


class Tiles:
    def __init__(self, first, tall):
        self.first, self.tall = first, tall

    def lines(self, half, piece):
        size = self.tall // 2
        if piece is None:
            return self.first + half * size, size
        return self.first + half * size + piece * (size // 2), size // 2

    def part(self, ref, spot_of, half, piece):
        z, y = spot_of
        first, count = self.lines(half, piece)
        start = pl.multiple_of(z * QB + first, count)
        return ref.at[pl.ds(start, count), span(y, DEEP)]


AXES = (("y", "z"), ("z", "y"))


class Gather:
    COUNT = 40

    def __init__(self, place, full, blocks, send, recv, own=None):
        self.place, self.full, self.blocks = place, full, blocks
        self.send, self.recv, self.own = send, recv, own
        self.copies = []
        self.waited = set()
        self.table = {}

    def _part(self, offset, half, piece):
        return self.blocks.part(self.full, off(self.place, offset), half, piece)

    def _send(self, half, axis, sign, offset, piece):
        index = len(self.copies)
        move = shift(axis, sign)
        block = self._part(offset, half, piece)
        source = block
        if offset == (0, 0) and self.own is not None:
            source = self.own.at[pl.ds(*self.blocks.lines(half, piece)), :]
        copy = pltpu.make_async_remote_copy(
            src_ref=source,
            dst_ref=block,
            send_sem=self.send.at[index],
            recv_sem=self.recv.at[index],
            device_id=at(self.place, *move),
            device_id_type=MESH,
        )
        copy.start()
        self.copies.append(copy)
        landed = (offset[0] - move[0], offset[1] - move[1])
        norm = tuple(2 if v == -2 else v for v in landed)
        self.table.setdefault((half, norm), []).append((index, landed, piece))

    def need(self, half, offset):
        for index, landed, piece in self.table.get((half, offset), ()):
            if index in self.waited:
                continue
            self.waited.add(index)
            block = self._part(landed, half, piece)
            pltpu.make_async_remote_copy(
                src_ref=block,
                dst_ref=block,
                send_sem=self.send.at[index],
                recv_sem=self.recv.at[index],
                device_id=at(self.place, 0, 1),
                device_id_type=MESH,
            ).wait_recv()

    def steps(self):
        for half, (a, b) in enumerate(AXES):
            for sign in (1, -1):
                self._send(half, a, sign, (0, 0), None)
        for half, (a, b) in enumerate(AXES):
            for sign in (1, -1):
                self._send(half, b, sign, (0, 0), None)
        yield 0
        for half, (a, b) in enumerate(AXES):
            for sign in (1, -1):
                offset = shift(a, -sign)
                self.need(half, offset)
                self._send(half, a, sign, offset, 0 if sign == 1 else 1)
                for along in (1, -1):
                    self._send(half, b, along, offset, None)
        yield 1
        for half, (a, b) in enumerate(AXES):
            for sign in (1, -1):
                offset = shift(b, -sign)
                self.need(half, offset)
                self._send(half, b, sign, offset, 0 if sign == 1 else 1)
        yield 2
        for half, (a, b) in enumerate(AXES):
            offset = shift(a, 2)
            self.need(half, offset)
            for along in (1, -1):
                self._send(half, b, along, offset, None)
        yield 3
        for half, (a, b) in enumerate(AXES):
            for o in (1, -1):
                for sign in (1, -1):
                    offset = plus(shift(a, o), shift(b, -sign))
                    self.need(half, offset)
                    self._send(half, b, sign, offset, 0 if sign == 1 else 1)
        yield 4
        for half, (a, b) in enumerate(AXES):
            for sign in (1, -1):
                offset = plus(shift(a, 2), shift(b, -sign))
                self.need(half, offset)
                self._send(half, b, sign, offset, 0 if sign == 1 else 1)
        yield 5

    def finish(self):
        for half, offset in list(self.table):
            self.need(half, offset)
        for copy in self.copies:
            copy.wait_send()


class Scatter:
    COUNT = 40

    def __init__(self, place, part, blocks, halves, quarters, send, recv):
        self.place, self.part, self.blocks = place, part, blocks
        self.halves, self.quarters, self.send, self.recv = halves, quarters, send, recv
        self.copies = []
        self.counts = [0, 0]
        self.landed = {}
        self.results = []

    def _here(self, offset, half, piece):
        return self.blocks.part(self.part, off(self.place, offset), half, piece)

    def _send(self, half, axis, sign, offset, piece, key):
        index = len(self.copies)
        kind = 0 if piece is None else 1
        land = (self.halves if kind == 0 else self.quarters).at[self.counts[kind]]
        self.counts[kind] += 1
        copy = pltpu.make_async_remote_copy(
            src_ref=self._here(offset, half, piece),
            dst_ref=land,
            send_sem=self.send.at[index],
            recv_sem=self.recv.at[index],
            device_id=at(self.place, *shift(axis, sign)),
            device_id_type=MESH,
        )
        copy.start()
        self.copies.append(copy)
        self.landed[key] = (copy, land)

    def _take(self, key):
        copy, land = self.landed[key]
        copy.wait_recv()
        return land[...]

    def _three(self, half, offset, name):
        summed = self._here(offset, half, None)[...].astype(F32)
        there = self._take((name, half, 1, "h")).astype(F32)
        return summed + (there + self._take((name, half, -1, "h")).astype(F32))

    def _line(self, half, axis, base, name):
        for sign in (1, -1):
            offset = plus(base, shift(axis, 2 * sign))
            piece = 0 if sign == 1 else 1
            self._send(half, axis, sign, offset, piece, (name, half, sign, "q"))

    def _pass(self, half, axis, base, name):
        for sign in (1, -1):
            offset = plus(base, shift(axis, sign))
            here = self._here(offset, half, 0 if sign == 1 else 1)
            here[...] = here[...] + self._take((name, half, sign, "q"))
            self._send(half, axis, sign, offset, None, (name, half, sign, "h"))

    def steps(self):
        outer = (2, 1, -1, 0)
        for o in outer:
            for half, (a, b) in enumerate(AXES):
                self._line(half, b, shift(a, o), o)
        yield 0
        for o in outer:
            for half, (a, b) in enumerate(AXES):
                self._pass(half, b, shift(a, o), o)
            yield 1
        for half, (a, b) in enumerate(AXES):
            summed = self._three(half, shift(a, 2), 2)
            self._here(shift(a, 2), half, None)[...] = summed.astype(BF16)
            self._line(half, a, (0, 0), "own")
        yield 2
        for half, (a, b) in enumerate(AXES):
            for sign in (1, -1):
                summed = self._three(half, shift(a, sign), sign)
                self._here(shift(a, sign), half, None)[...] = summed.astype(BF16)
        yield 3
        for half, (a, b) in enumerate(AXES):
            self._pass(half, a, (0, 0), "own")
        yield 4
        for half, (a, b) in enumerate(AXES):
            summed = self._three(half, (0, 0), 0)
            there = self._take(("own", half, 1, "h")).astype(F32)
            there = there + self._take(("own", half, -1, "h")).astype(F32)
            self.results.append((self.blocks.lines(half, None), summed + there))
        yield 5

    def finish(self):
        for copy in self.copies:
            copy.wait_send()


class Along:
    def __init__(self, axis, place=None):
        self.axis, self.place = axis, place
        self.me = lax.axis_index("dp") if axis == "dp" else place["zy".index(axis)]

    def peer(self, step):
        if self.axis == "dp":
            return beside(step)
        return at(self.place, *shift(self.axis, step))

    def pos(self, step):
        return wrap(self.me + step)


class RingGather:
    def __init__(self, copies, along, pieces):
        self.copies, self.along, self.pieces = copies, along, pieces

    def start(self):
        along = self.along
        self.first = [
            [self.copies.to(along.peer(s), p, p) for p in self.pieces(along.me, None)]
            for s in (1, -1)
        ]

    def relay(self, arrived=None):
        along = self.along
        self.second = []
        for n, s in enumerate((1, -1)):
            for copy in self.first[n]:
                copy.wait_recv()
            came = along.pos(-s)
            self.second += [self.copies.to(along.peer(s), p, p) for p in self.pieces(came, n)]
            if arrived is not None:
                arrived(came)

    def finish(self, arrived=None):
        for copy in self.second:
            copy.wait_recv()
        if arrived is not None:
            arrived(self.along.pos(2))


class RingScatter:
    def __init__(self, copies, along, pieces, halves, fulls):
        self.copies, self.along, self.pieces = copies, along, pieces
        self.halves, self.fulls = halves, fulls

    def start(self):
        along = self.along
        self.first = [
            [
                self.copies.to(along.peer(s), p, land)
                for p, land in zip(self.pieces(along.pos(2), n), self.halves[n], strict=True)
            ]
            for n, s in enumerate((1, -1))
        ]

    def relay(self):
        along = self.along
        self.second = []
        for n, s in enumerate((1, -1)):
            targets = self.pieces(along.pos(s), n)
            for copy, target, land in zip(self.first[n], targets, self.halves[n], strict=True):
                copy.wait_recv()
                target[...] = target[...] + land[...]
            for p, land in zip(self.pieces(along.pos(s), None), self.fulls[n], strict=True):
                self.second.append(self.copies.to(along.peer(s), p, land))

    def wait(self):
        for copy in self.second:
            copy.wait_recv()

    def total(self, index=0):
        there = self.fulls[0][index][...].astype(F32) + self.fulls[1][index][...].astype(F32)
        return self.pieces(self.along.me, None)[index][...].astype(F32) + there


class AxisTotals:
    def __init__(self, place, own, slots, send, recv):
        self.own, self.slots = own, slots
        self.copies = Copies(send, recv)
        for i, step in enumerate((1, -1, 2)):
            self.copies.to(at(place, 0, step), own, slots.at[i])

    def finish(self):
        for copy in self.copies.open:
            copy.wait_recv()
        self.copies.finish()
        return (self.own[...] + self.slots[2]) + (self.slots[0] + self.slots[1])


class Totals:
    def __init__(self, place, own, mid, slots, send, recv):
        self.place, self.own, self.mid, self.slots = place, own, mid, slots
        self.send, self.recv = send, recv
        self.open = []

    def _start(self, axis, source, base):
        for i, step in enumerate((1, -1, 2)):
            copy = pltpu.make_async_remote_copy(
                src_ref=source,
                dst_ref=self.slots.at[base + i],
                send_sem=self.send.at[base + i],
                recv_sem=self.recv.at[base + i],
                device_id=at(self.place, *shift(axis, step)),
                device_id_type=MESH,
            )
            copy.start()
            self.open.append(copy)

    def first(self):
        self._start("y", self.own, 0)

    def second(self):
        for copy in self.open[:3]:
            copy.wait_recv()
        self.mid[...] = (self.own[...] + self.slots[2]) + (self.slots[0] + self.slots[1])
        self._start("z", self.mid, 3)

    def finish(self):
        for copy in self.open[3:]:
            copy.wait_recv()
        total = (self.mid[...] + self.slots[5]) + (self.slots[3] + self.slots[4])
        for copy in self.open:
            copy.wait_send()
        return total


def nt(left, right):
    return lax.dot_general(left, right, (((1,), (1,)), ((), ())), preferred_element_type=F32)


def tn(left, right):
    return lax.dot_general(left, right, (((0,), (0,)), ((), ())), preferred_element_type=F32)


def nn(left, right):
    return jnp.dot(left, right, preferred_element_type=F32)


def lane(shape):
    return lax.broadcasted_iota(jnp.int32, shape, 1)


def turn(values, cosine, sine):
    width = values.shape[1]
    half = HS // 2
    other = jnp.where(
        lane(values.shape) % HS < half,
        pltpu.roll(values, width - half, 1),
        pltpu.roll(values, half, 1),
    )
    return values * cosine + other * sine


def row_sums(values):
    ones = jnp.ones((8, values.shape[1]), F32)
    return lax.dot_general(
        ones,
        values,
        (((1,), (1,)), ((), ())),
        precision=lax.Precision.HIGHEST,
        preferred_element_type=F32,
    )


def gain_row(gains, which):
    return jnp.concatenate([gains[k][which : which + 1] for k in range(SIDE)], axis=1)


VMEM = pl.BlockSpec(memory_space=pltpu.VMEM)
SMEM = pl.BlockSpec(memory_space=pltpu.SMEM)
ANY = pl.BlockSpec(memory_space=pl.ANY)


def dma(count):
    return pltpu.SemaphoreType.DMA((count,))


def shape(dims, dtype=BF16):
    return jax.ShapeDtypeStruct(dims, dtype)


def launch(kernel, ident, inputs, outs, scratch):
    names = list(inputs) + list(outs) + list(scratch)

    def body(*refs):
        kernel(types.SimpleNamespace(**dict(zip(names, refs, strict=True))))

    results = pl.pallas_call(
        body,
        out_shape=tuple(out for out, _ in outs.values()),
        in_specs=[spec for _, spec in inputs.values()],
        out_specs=tuple(spec for _, spec in outs.values()),
        scratch_shapes=list(scratch.values()),
        compiler_params=pltpu.CompilerParams(
            collective_id=ident, has_side_effects=True, vmem_limit_bytes=60 * MIB
        ),
        name=kernel.__name__,
    )(*(array for array, _ in inputs.values()))
    return types.SimpleNamespace(**dict(zip(outs, results, strict=True)))


def allowed(start):
    key = lax.broadcasted_iota(jnp.int32, (QB, WIN), 1)
    query = LONGEST + lax.broadcasted_iota(jnp.int32, (QB, WIN), 0)
    return (key >= start) & (key <= query)


def probabilities(query, keys, ok):
    scores = jnp.where(ok, nt(query, keys) * HS**-0.5, -1e30)
    expo = jnp.exp(scores - jnp.max(scores, axis=1, keepdims=True))
    return expo * (1.0 / jnp.sum(expo, axis=1, keepdims=True))


def attend_pair(r, j):
    ok = allowed(r.start[...])
    window = r.kvs[lax.div(j, 2)]
    keys, values = window[:, :HS], window[:, HS:]
    queries = r.q[:, span(j, WIDE)]
    both = []
    for h in range(2):
        probs = probabilities(queries[:, h * HS : (h + 1) * HS], keys, ok).astype(BF16)
        both.append(nn(probs, values))
    r.heads[:, span(j, WIDE)] = jnp.concatenate(both, axis=1).astype(BF16)


def attend_pair_back(r, j):
    ok = allowed(r.start[...])
    side = lax.div(j, 2)
    window = r.kvs[side]
    keys, values = window[:, :HS], window[:, HS:]
    queries, grads = r.q[:, span(j, WIDE)], r.gheads[:, span(j, WIDE)]
    both = []
    key_sum = value_sum = None
    for h in range(2):
        query, grad = queries[:, h * HS : (h + 1) * HS], grads[:, h * HS : (h + 1) * HS]
        probs = probabilities(query, keys, ok)
        grad_probs = nt(grad, values)
        delta = jnp.sum(probs * grad_probs, axis=1, keepdims=True)
        grad_scores = (probs * (grad_probs - delta)).astype(BF16)
        both.append(nn(grad_scores, keys) * HS**-0.5)
        key_term = tn(grad_scores, query) * HS**-0.5
        value_term = tn(probs.astype(BF16), grad)
        key_sum = key_term if h == 0 else key_sum + key_term
        value_sum = value_term if h == 0 else value_sum + value_term
    r.dq[:, span(j, WIDE)] = jnp.concatenate(both, axis=1)
    r.dkv[side] = r.dkv[side] + jnp.concatenate([key_sum, value_sum], axis=1)


def out_weights(r, n):
    return jnp.concatenate([r.w_out[n, k].reshape(-1, WIDE) for k in range(SIDE)], axis=1)


AHEAD_PLAN = (
    "ovwkovw",
    "",
    "o",
    "b",
    "",
    "vwcovw",
    "ao",
    "",
    "",
    "ock",
    "",
    "akb",
    "",
    "",
    "",
    "ka",
    "k",
    "ak",
    "1c21",
    "21b1",
    "",
    "12a",
    "bc1",
    "22",
    "",
    "2",
    "",
    "",
    "3",
    "33",
    "33",
    "3",
    "4",
    "f4e43",
    "44ff43e",
    "4e",
    "4ef",
)


def front(r, place, plan, local):
    z, y = place
    core = lax.axis_index("row")
    quarter = lax.axis_index("dp")
    depth = r.wg.shape[0]
    width = COLS * depth
    unit = r.wd.shape[0] // COLS
    share, tall = depth // SIDE, unit // SIDE
    half = depth // 2
    strip = r.strips.shape[1]
    nq, nk = r.wq.shape[1], r.wk.shape[1]
    count = hail(place, wide=True)
    misc, deals, flows = Copies(r.ms, r.mr), Copies(r.bs, r.br), Copies(r.ws, r.wr)
    spot_of = y * SIDE + z
    along_y, along_z, along_dp = Along("y", place), Along("z", place), Along("dp")

    def dealt(ref, which):
        return ref.at[span(which, half), :]

    def dealt_out(n, which):
        first = n * (r.wo.shape[0] // 2) + (quarter * 2 + which) * strip
        return r.wo.at[pl.ds(pl.multiple_of(first, strip), strip), :]

    parts = ((r.wq, 0, nq), (r.wk, nq, nk), (r.wv, nq + nk, nk))
    kept = [
        local.move(dealt(ref, core), r.mine.at[:, pl.ds(first, size)])
        for ref, first, size in parts
    ]
    kept_x = local.move(r.x.at[span(z, QB), :], r.xt.at[:, span(z, WIDE)])
    kept_out = [local.move(dealt_out(n, core), r.strips.at[2 * core + n]) for n in range(2)]
    kept_cot = local.move(r.cot, r.cots.at[:, span(spot_of, WIDE)])
    row = lax.broadcasted_iota(jnp.int32, (8, WIDE), 0)
    one = r.gain_one[...].astype(F32).reshape(1, WIDE)
    two = r.gain_two[...].astype(F32).reshape(1, WIDE)
    r.gains[z] = jnp.where(row == 0, one, two)
    meet(count)
    swaps = [
        misc.to(other_core(), dealt(ref, 1 - core), r.theirs.at[:, pl.ds(first, size)])
        for ref, first, size in parts
    ]
    x_moves = []
    for k in (1, -1, 2):
        to = wrap(z + k)
        x_moves.append(
            misc.to(at(place, k, 0), r.x.at[span(to, QB), :], r.xt.at[:, span(z, WIDE)])
        )
        x_moves.append(misc.to(at(place, k, 0), r.gains.at[z], r.gains.at[z]))
    out_swaps = [
        misc.to(other_core(), dealt_out(n, 1 - core), r.strips.at[2 * core + n]) for n in range(2)
    ]

    def gate_cut(ref, chips, pos):
        return ref.at[core, chips, pos, :, pl.ds(0, unit)]

    def up_cut(ref, chips, pos):
        return ref.at[core, chips, pos, :, pl.ds(unit, unit)]

    def cross(pieces):
        return [misc.to(other_core(), p, p) for p in pieces]

    def spread(ring, pieces, me):
        crossing = []
        arrived = lambda pos: crossing.extend(cross(pieces(pos, None)))
        ring.start()
        arrived(me)
        yield 1
        ring.relay(arrived)
        yield 2
        ring.finish(arrived)
        yield 3
        for copy in crossing:
            copy.wait_recv()
        yield 4

    def feed_flow(which):
        waits = []
        mine_rows = span(quarter, share)
        for k in range(COLS):
            to = chip(k)
            if which == 0:
                source = r.wg.at[mine_rows, span(to, unit)]
                target = gate_cut(r.gu, spot_of, quarter)
            elif which == 1:
                source = r.wu.at[mine_rows, span(to, unit)]
                target = up_cut(r.gu, spot_of, quarter)
            else:
                down_rows = pl.ds(pl.multiple_of(to * unit + quarter * tall, tall), tall)
                source = r.wd.at[down_rows, :]
                target = r.d.at[core, quarter, :, span(spot_of, depth)]
            if k == 0:
                waits.append(local.move(source, target).wait)
            else:
                waits.append(deals.to({"col": to}, source, target).wait_recv)
        yield 0

        def pieces(pos, part):
            chips = pl.ds(0, COLS) if part is None else pl.ds(part * (COLS // 2), COLS // 2)
            if which == 0:
                return [gate_cut(r.gu, chips, pos)]
            if which == 1:
                return [up_cut(r.gu, chips, pos)]
            rows = pl.ds(0, tall) if part is None else pl.ds(part * (tall // 2), tall // 2)
            return [r.d.at[core, pos, rows, :]]

        for wait in waits:
            wait()
        yield from spread(RingGather(flows, along_dp, pieces), pieces, quarter)

    def multicast(blocks, ref):
        sends = [
            misc.to(at(place, 0, k), blocks.at[wrap(y + k)], ref.at[y, z, quarter, core])
            for k in (1, -1, 2)
        ]
        ref[y, z, quarter, core] = blocks[y]
        yield 0
        for copy in sends:
            copy.wait_recv()

        def lead(part):
            return pl.ds(0, SIDE) if part is None else pl.ds(part * 2, 2)

        ring = RingGather(
            misc, along_z, lambda pos, part: [ref.at[lead(part), pos, quarter, core]]
        )
        ring.start()
        yield 1
        ring.relay()
        yield 2
        ring.finish()
        pieces = lambda pos, part: [ref.at[lead(part), :, pos, core]]
        yield from spread(RingGather(misc, along_dp, pieces), pieces, quarter)

    prepared = []

    def prepare():
        if prepared:
            return
        prepared.append(True)
        for copy in kept:
            copy.wait()
        for copy in swaps:
            copy.wait_recv()
        own, got = r.mine[...], r.theirs[...]
        sides = (jnp.where(core == 0, own, got), jnp.where(core == 0, got, own))
        for group in range(SIDE):
            side, n = sides[group // 2], group % 2
            pieces = []
            for kv in range(KVS):
                first = (n * KVS + kv) * HS
                pieces.append(side[:, nq + first : nq + first + HS])
                pieces.append(side[:, nq + nk + first : nq + nk + first + HS])
            r.blocks_kv[group] = jnp.concatenate(pieces, axis=1)
            r.blocks_q[group] = side[:, n * HEADS * HS : (n + 1) * HEADS * HS]

    def head_flow(blocks, ref):
        prepare()
        sends = [
            misc.to(at(place, 0, k), blocks.at[wrap(y + k)], ref.at[y, z, core])
            for k in (1, -1, 2)
        ]
        ref[y, z, core] = blocks[y]
        yield 0
        for copy in sends:
            copy.wait_recv()

        def pieces(pos, part):
            lead = pl.ds(0, SIDE) if part is None else pl.ds(part * 2, 2)
            return [ref.at[lead, pos, core]]

        yield from spread(RingGather(misc, along_z, pieces), pieces, z)

    def out_flow():
        for copy in kept_out:
            copy.wait()
        for copy in out_swaps:
            copy.wait_recv()
        yield from multicast(r.strips, r.w_out)

    def angle_flow():
        base = (core * SIDE + z) * QB
        index = base + lax.broadcasted_iota(jnp.int32, (QB, WIDE), 0)
        begin = jnp.zeros((QB, WIDE), jnp.int32)
        first = jnp.int32(0)
        for s in range(r.lengths.shape[1]):
            begin = jnp.where(index >= first, jnp.maximum(begin, first), begin)
            first = first + r.lengths[0, s]
        r.start[...] = begin[:, :1] - (base - LONGEST)
        lanes = lane((QB, WIDE))
        freqs = jnp.exp((lanes % (HS // 2)).astype(F32) * (-2.0 * 13.122363377404328 / HS))
        turned = (index - begin).astype(F32) * freqs
        r.cos[...] = jnp.cos(turned)
        sine = jnp.sin(turned)
        r.sin[...] = jnp.where(lanes % HS < HS // 2, -sine, sine)
        yield 0

    gather = Gather(place, r.cots, Slabs(r.cot.shape[0]), r.gs, r.gr, own=r.cot)

    def cot_flow():
        yield from gather.steps()
        kept_cot.wait()
        gather.finish()
        yield 6

    plan.add("a", feed_flow(0))
    plan.add("b", feed_flow(1))
    plan.add("c", feed_flow(2))
    plan.add("v", head_flow(r.blocks_kv, r.w_kv))
    plan.add("w", head_flow(r.blocks_q, r.w_q))
    plan.add("o", out_flow())
    plan.add("t", angle_flow())
    plan.add("k", cot_flow())
    plan.point()

    kept_x.wait()
    plan.point()
    for copy in x_moves:
        copy.wait_recv()
    x = r.xt[...].astype(F32)
    r.x_all[:, span(y, DEEP)] = (x * gain_row(r.gains, 0)).astype(BF16)

    def rows_of(ref):
        def pieces(pos, part):
            rows = pl.ds(0, QB) if part is None else pl.ds(part * (QB // 2), QB // 2)
            return [ref.at[rows, span(pos, DEEP)]]

        return pieces

    x_ring = RingGather(misc, along_y, rows_of(r.x_all))
    x_ring.start()
    r.stat[...] = row_sums(x * x)
    square = AxisTotals(place, r.stat, r.slots, r.ts, r.tr)
    plan.point()
    plan.point()
    x_ring.relay()
    plan.point()
    plan.point()
    x_ring.finish()
    rms = lax.rsqrt(jnp.transpose(square.finish())[:, :1] / width + EPS)
    r.rms[...] = rms
    plan.point()
    plan.drain("tv")
    plan.point()

    cosine, sine = r.cos[...], r.sin[...]

    def project(weights, first):
        columns = slice(first, first + QB)
        raw = nn(r.x_all[...], weights.reshape(width, QB)) * rms
        r.raw[:, columns] = raw
        return [
            (raw[:, m * WIDE : (m + 1) * WIDE], turn(raw[:, m * WIDE : (m + 1) * WIDE], cosine, sine))
            for m in range(2)
        ]

    for m, (plain, rotated) in enumerate(project(r.w_kv[...], HEADS * HS)):
        kv = jnp.where(lane(plain.shape) < HS, rotated, plain)
        r.kvs[m, LONGEST:, :] = kv.astype(BF16)
    halo = [
        misc.to(
            tile_peer(place, k),
            r.kvs.at[side, pl.ds(LONGEST, QB), :],
            r.kvs.at[side, pl.ds(LONGEST - k * QB, QB), :],
        )
        for side in range(KVS)
        for k in (1, 2)
    ]
    plan.point()
    plan.drain("w")
    for n in range(2):
        pairs = project(r.w_q[..., n * QB : (n + 1) * QB], n * QB)
        for m, (_, rotated) in enumerate(pairs):
            first = (2 * n + m) * WIDE
            r.q[:, first : first + WIDE] = rotated.astype(BF16)
    plan.point()
    for j in range(SIDE):
        if j % 2 == 0:
            for copy in halo[j : j + 2]:
                copy.wait_recv()
        plan.point()
        attend_pair(r, jnp.int32(j))
    plan.point()
    plan.drain("o")

    heads = r.heads[...]
    for n in range(SIDE):
        r.terms[:, pl.ds(n * DEEP, DEEP)] = nn(heads, out_weights(r, n)).astype(BF16)
    term_ring = RingScatter(
        misc,
        along_y,
        rows_of(r.terms),
        [[r.half_terms.at[n]] for n in range(2)],
        [[r.full_terms.at[n]] for n in range(2)],
    )
    term_ring.start()
    plan.point()
    term_ring.relay()
    plan.point()
    plan.point()
    term_ring.wait()
    r.hidden[...] = r.xt[...].astype(F32) + term_ring.total()
    for name in ("xt", "x_all", "heads", "hidden", "raw", "q", "kvs", "rms", "cos", "sin"):
        local.move(getattr(r, name), getattr(r, name + "_out"))
    for name in ("start", "gains", "w_q", "w_kv", "w_out"):
        local.move(getattr(r, name), getattr(r, name + "_out"))
    return misc, deals, flows


def take(ref, chunk, columns=slice(None)):
    size = QB // 2
    pieces = [
        ref[n * QB + chunk * size : n * QB + (chunk + 1) * size, columns] for n in range(SIDE)
    ]
    return jnp.concatenate(pieces, axis=0)


def put(ref, chunk, values, columns=slice(None)):
    size = QB // 2
    for n in range(SIDE):
        rows = slice(n * QB + chunk * size, n * QB + (chunk + 1) * size)
        ref[rows, columns] = values[n * size : (n + 1) * size]


def feed_chunk(r, chunk):
    unit = r.act.shape[1] // 2
    rms = take(r.rms2, chunk)
    left = take(r.normed, chunk)
    dots = None
    for side in range(2):
        columns = slice(side * unit, (side + 1) * unit)
        both = nn(left, r.gu[side].reshape(COLS * WIDE, -1)) * rms
        gate, up = both[:, :unit], both[:, unit:]
        sigma = 1.0 / (1.0 + jnp.exp(-gate))
        swish = gate * sigma
        put(r.act, chunk, (swish * up).astype(BF16), columns)
        grad_act = take(r.grad_act, chunk, columns)
        grad_gate = grad_act * up * sigma * (1.0 + gate * (1.0 - sigma))
        grad_up = grad_act * swish
        term = grad_gate * gate + grad_up * up
        dots = term if side == 0 else dots + term
        grads = jnp.concatenate([grad_gate, grad_up], axis=1)
        columns = slice(2 * side * unit, 2 * (side + 1) * unit)
        put(r.grads, chunk, (grads * rms).astype(BF16), columns)
        r.plain[:, columns] = grads.astype(BF16)
        yield side
    for n in range(SIDE):
        columns = slice(n * DEEP, (n + 1) * DEEP)
        rows = pl.ds(n * SIDE, SIDE)
        weights = [r.gu[side, rows].reshape(DEEP, -1) for side in range(2)]
        part = nt(r.plain[...], jnp.concatenate(weights, axis=1))
        put(r.part, chunk, part.astype(BF16), columns)
        if n % 2 == 1:
            yield 1 + n
    sums = row_sums(dots)
    size = QB // 2
    for n in range(SIDE):
        lanes = slice(n * QB + chunk * size, n * QB + (chunk + 1) * size)
        r.stat2[:, lanes] = sums[:, n * size : (n + 1) * size]


def middle(r, place, plan, local):
    z, y = place
    width = COLS * WIDE
    unit = r.act.shape[1] // 2
    down = lambda columns: r.d[:, :, :, columns].reshape(2 * unit, -1)
    chunk = QB // 2
    gain = gain_row(r.gains, 1)
    hidden = r.hidden[...]
    r.normed[span(z, QB), span(y, DEEP)] = (hidden * gain).astype(BF16)
    gathers = [
        Gather(place, r.normed, Tiles(n * chunk, chunk), send, recv)
        for n, (send, recv) in enumerate(((r.gs0, r.gr0), (r.gs1, r.gr1)))
    ]

    def pull_flow():
        for i in range(2):
            here = pl.ds(2 * i * QB, 2 * QB)
            r.grad_act[here, :] = nt(r.cots[here, :], down(slice(None)))
            yield i

    plan.add("1", gathers[0].steps())
    plan.add("2", gathers[1].steps())
    plan.point()
    r.stat1[...] = row_sums(hidden * hidden)
    square = AxisTotals(place, r.stat1, r.slots1, r.ts1, r.tr1)
    plan.point()
    own = r.stats.at[:, span(z, QB)]
    own[...] = square.finish()
    shares = Copies(r.zs, r.zr)
    for k in (1, -1, 2):
        shares.to(at(place, k, 0), own, own)
    plan.point()
    plan.point()
    plan.point()
    plan.point()
    for copy in shares.open:
        copy.wait_recv()
    r.rms2[...] = lax.rsqrt(jnp.transpose(r.stats[...])[:, :1] / width + EPS)
    plan.drain("ck")
    local.move(r.d, r.d_out)
    plan.add("p", pull_flow())
    plan.point()
    plan.drain("p1ab")
    gathers[0].finish()
    for n in feed_chunk(r, 0):
        if n != 1:
            plan.point()
    scatters = [
        Scatter(place, r.part, Tiles(n * chunk, chunk), halves, quarters, send, recv)
        for n, (halves, quarters, send, recv) in enumerate(
            (
                (r.halves0, r.quarters0, r.ss0, r.sr0),
                (r.halves1, r.quarters1, r.ss1, r.sr1),
            )
        )
    ]
    plan.add("3", scatters[0].steps())
    plan.point()
    plan.drain("2")
    gathers[1].finish()
    for n in feed_chunk(r, 1):
        if n == SIDE:
            plan.add("4", scatters[1].steps())
        plan.point()
    sums = Totals(place, r.stat2, r.mid2, r.slots2, r.ts2, r.tr2)
    sums.first()


    def both_flow():
        for b in range(SIDE):
            four = tn(r.normed[:, pl.ds(b * DEEP, DEEP)], r.grads[...])
            here = pl.ds(SIDE * b, SIDE)
            r.gu_sum[here] = four.astype(BF16).reshape(SIDE, *r.gu_sum.shape[1:])
            local.move(r.gu_sum.at[here], r.gu_grad.at[here])
            yield b

    def down_flow():
        for n in range(SIDE):
            columns = pl.ds(n * DEEP, DEEP)
            block = tn(r.act[...], r.cots[:, columns])
            r.d_sum[:, :, :, columns] = block.astype(BF16).reshape(*r.d_sum.shape[:3], DEEP)
            if n == SIDE - 1:
                local.move(r.d_sum, r.d_grad)
            yield n

    plan.add("e", both_flow())
    plan.add("f", down_flow())
    local.move(r.act, r.act_out)
    plan.point()
    plan.point()
    sums.second()
    plan.point()
    plan.point()
    plan.drain("3ef4")
    r.stat2[...] = sums.finish()
    mean = jnp.transpose(r.stat2[:, span(z, QB)])[:, :1] / width
    gain_sum = jnp.zeros((1, DEEP), F32)
    for scatter in scatters:
        for (first, size), summed in scatter.results:
            here = pl.ds(first, size)
            there = pl.ds(pl.multiple_of(z * QB + first, size), size)
            rms = r.rms2[there, :]
            xhat = r.hidden[here, :] * rms
            gain_sum = gain_sum + jnp.sum(summed * xhat, axis=0, keepdims=True)
            r.grad[here, :] = r.cots[there, span(y, DEEP)].astype(F32) + rms * (
                gain * summed - xhat * mean[first : first + size]
            )
    r.gain_two_out[...] = gain_sum
    shares.finish()
    for scatter in scatters:
        scatter.finish()


def ahead(r):
    place = spot()
    plan = Plan(AHEAD_PLAN)
    local = Locals(r.local)
    groups = front(r, place, plan, local)
    kept = len(local.open) - 15
    middle(r, place, plan, local)
    for copy in local.open[kept:]:
        copy.wait()
    for group in groups:
        group.finish()


def call_ahead(x, gain_one, gain_two, cot, wq, wk, wv, wo, wg, wu, wd, lengths):
    rows, depth = x.shape
    wide = COLS * depth
    unit = wd.shape[0] // COLS
    share, tall = depth // SIDE, unit // SIDE
    strip = wo.shape[0] // 16
    inputs = dict(x=x, gain_one=gain_one, gain_two=gain_two, cot=cot, wq=wq, wk=wk, wv=wv)
    inputs.update(wo=wo, wg=wg, wu=wu, wd=wd, lengths=lengths)
    inputs = {name: (array, ANY) for name, array in inputs.items()}
    inputs["gain_one"] = (gain_one, VMEM)
    inputs["gain_two"] = (gain_two, VMEM)
    inputs["lengths"] = (lengths, SMEM)
    kept = dict(
        xt=shape((QB, DEEP)),
        x_all=shape((QB, wide)),
        heads=shape((QB, HEADS * HS)),
        hidden=shape((QB, DEEP), F32),
        raw=shape((QB, HEAD_WIDTH), F32),
        q=shape((QB, HEADS * HS)),
        kvs=shape((KVS, WIN, 2 * HS)),
        rms=shape((QB, 1), F32),
        cos=shape((QB, WIDE), F32),
        sin=shape((QB, WIDE), F32),
        start=shape((QB, 1), jnp.int32),
        gains=shape((SIDE, 8, WIDE), F32),
        w_q=shape((SIDE, SIDE, 2, depth // 2, HEADS * HS)),
        w_kv=shape((SIDE, SIDE, 2, depth // 2, 2 * KVS * HS)),
        w_out=shape((SIDE, SIDE, SIDE, 2, strip, depth)),
    )
    gu_shape = (COLS, SIDE, share, 4 * unit)
    d_shape = (2, SIDE, tall, wide)
    outs = {name + "_out": (value, ANY) for name, value in kept.items()}
    outs.update(
        grad=(shape((QB, DEEP), F32), VMEM),
        gain_two_out=(shape((1, DEEP), F32), VMEM),
        act_out=(shape((rows, 2 * unit)), ANY),
        d_out=(shape(d_shape), ANY),
        gu_grad=(shape(gu_shape), ANY),
        d_grad=(shape(d_shape), ANY),
    )
    scratch = {name: pltpu.VMEM(value.shape, value.dtype) for name, value in kept.items()}
    scratch.update(
        mine=pltpu.VMEM((depth // 2, wq.shape[1] + 2 * wk.shape[1]), BF16),
        theirs=pltpu.VMEM((depth // 2, wq.shape[1] + 2 * wk.shape[1]), BF16),
        blocks_q=pltpu.VMEM((SIDE, depth // 2, HEADS * HS), BF16),
        blocks_kv=pltpu.VMEM((SIDE, depth // 2, 2 * KVS * HS), BF16),
        strips=pltpu.VMEM((SIDE, strip, depth), BF16),
        terms=pltpu.VMEM((QB, wide), BF16),
        half_terms=pltpu.VMEM((2, QB // 2, DEEP), BF16),
        full_terms=pltpu.VMEM((2, QB, DEEP), BF16),
        stat=pltpu.VMEM((8, QB), F32),
        slots=pltpu.VMEM((3, 8, QB), F32),
        stat1=pltpu.VMEM((8, QB), F32),
        slots1=pltpu.VMEM((3, 8, QB), F32),
        normed=pltpu.VMEM((rows, wide), BF16),
        gu=pltpu.VMEM((2, COLS, SIDE, share, 2 * unit), BF16),
        d=pltpu.VMEM(d_shape, BF16),
        cots=pltpu.VMEM((rows, wide), BF16),
        part=pltpu.VMEM((rows, wide), BF16),
        act=pltpu.VMEM((rows, 2 * unit), BF16),
        grads=pltpu.VMEM((rows, 4 * unit), BF16),
        grad_act=pltpu.VMEM((rows, 2 * unit), F32),
        plain=pltpu.VMEM((rows // 2, 4 * unit), BF16),
        gu_sum=pltpu.VMEM(gu_shape, BF16),
        d_sum=pltpu.VMEM(d_shape, BF16),
        rms2=pltpu.VMEM((rows, 1), F32),
        halves0=pltpu.VMEM((20, QB // 4, DEEP), BF16),
        quarters0=pltpu.VMEM((20, QB // 8, DEEP), BF16),
        halves1=pltpu.VMEM((20, QB // 4, DEEP), BF16),
        quarters1=pltpu.VMEM((20, QB // 8, DEEP), BF16),
        stats=pltpu.VMEM((8, rows), F32),
        stat2=pltpu.VMEM((8, rows), F32),
        mid2=pltpu.VMEM((8, rows), F32),
        slots2=pltpu.VMEM((6, 8, rows), F32),
    )
    for name, size in (("t", 3), ("g", Gather.COUNT), ("m", 96), ("b", 3 * (COLS - 1)), ("w", 12)):
        scratch[name + "s"] = dma(size)
        scratch[name + "r"] = dma(size)
    for name, size in (("1", 3), ("2", 6)):
        scratch["ts" + name] = dma(size)
        scratch["tr" + name] = dma(size)
    scratch["zs"] = dma(3)
    scratch["zr"] = dma(3)
    for name in ("gs0", "gr0", "gs1", "gr1", "ss0", "sr0", "ss1", "sr1"):
        scratch[name] = dma(Gather.COUNT)
    scratch["local"] = dma(48)
    return launch(ahead, 1, inputs, outs, scratch)


class FeedSum:
    def __init__(self, r, name):
        self.r, self.name = r, name
        self.core, self.me = lax.axis_index("row"), lax.axis_index("col")
        self.quarter = lax.axis_index("dp")
        for part in ("sum", "came", "half", "full"):
            setattr(self, part, getattr(r, f"{name}_{part}"))
        self.out = getattr(r, f"{name}_out")
        self.copies = Copies(getattr(r, f"{name}_send"), getattr(r, f"{name}_recv"))

    def _grad(self, core):
        r = self.r
        if self.name == "down":
            return r.d_grad.at[core]
        unit = self.sum.shape[3]
        first = core * 2 * unit + (unit if self.name == "up" else 0)
        return r.gu_grad.at[:, :, :, pl.ds(pl.multiple_of(first, unit), unit)]

    def _pieces(self, pos, part):
        if self.name == "down":
            tall = self.sum.shape[1]
            rows = pl.ds(0, tall) if part is None else pl.ds(part * (tall // 2), tall // 2)
            return [self.sum.at[pos, rows, :]]
        chips = pl.ds(0, COLS) if part is None else pl.ds(part * (COLS // 2), COLS // 2)
        return [self.sum.at[chips, pos]]

    def _outs(self, pos, part):
        if self.name == "down":
            chips = pl.ds(0, COLS) if part is None else pl.ds(part * (COLS // 2), COLS // 2)
            return [self.out.at[chips, pos]]
        size = self.out.shape[1]
        cut = pl.ds(0, size) if part is None else pl.ds(part * (size // 2), size // 2)
        return [self.out.at[span(pos, self.sum.shape[2]), cut]]

    def steps(self):
        g = self.quarter
        load = self.r.locals.move(self._grad(self.core), self.sum)
        swap = self.copies.to(other_core(), self._grad(1 - self.core), self.came)
        yield 0
        load.wait()
        swap.wait_recv()

        def add(i, carry):
            self.sum[i] = self.sum[i] + self.came[i]
            return carry

        lax.fori_loop(0, self.sum.shape[0], add, 0)
        ring = RingScatter(
            self.copies,
            Along("dp"),
            self._pieces,
            [[self.half.at[n]] for n in range(2)],
            [[self.full.at[n]] for n in range(2)],
        )
        ring.start()
        yield 1
        ring.relay()
        yield 2
        ring.wait()
        (mine,) = self._pieces(g, None)
        mine[...] = ring.total().astype(BF16)
        deals = []
        for k in range(COLS):
            c = chip(k)
            where = lax.rem(c, SIDE) * SIDE + lax.div(c, SIDE)
            if self.name == "down":
                source, target = mine.at[:, span(where, WIDE)], self.out.at[self.me, g]
            else:
                source = self.sum.at[where, g]
                target = self.out.at[span(g, self.sum.shape[2]), span(self.me, self.sum.shape[3])]
            if k == 0:
                deals.append(self.r.locals.move(source, target).wait)
            else:
                deals.append(self.copies.to({"col": c}, source, target).wait_recv)
        yield 3
        for wait in deals:
            wait()
        ring = RingGather(self.copies, Along("dp"), self._outs)
        ring.start()
        yield 4
        ring.relay()
        yield 5
        ring.finish()
        yield 6


class GroupSum:
    def __init__(self, r, place, name):
        self.place = place
        for part in ("grad", "sum", "half", "full", "part", "came", "own", "dealt", "out"):
            setattr(self, part, getattr(r, f"{name}_{part}"))
        self.copies = Copies(getattr(r, f"{name}_send"), getattr(r, f"{name}_recv"))

    def steps(self):
        z, y = place = self.place
        core, g = lax.axis_index("row"), lax.axis_index("dp")
        to = self.copies.to
        swap = to(other_core(), self.grad.at[:, :, 1 - core], self.sum)
        yield 0
        swap.wait_recv()

        def add(i, carry):
            self.sum[i] = self.sum[i] + self.grad[i, :, core]
            return carry

        lax.fori_loop(0, SIDE, add, 0)

        def pieces(pos, part):
            lead = pl.ds(0, SIDE) if part is None else pl.ds(part * 2, 2)
            return [self.sum.at[lead, pos]]

        ring = RingScatter(
            self.copies,
            Along("z", place),
            pieces,
            [[self.half.at[n]] for n in range(2)],
            [[self.full.at[n]] for n in range(2)],
        )
        ring.start()
        yield 1
        ring.relay()
        yield 2
        ring.wait()
        total = ring.total().astype(BF16)
        size = self.part.shape[2]
        for k in range(SIDE):
            self.part[k] = total[:, k * size : (k + 1) * size]
        sends = [
            to(beside(k), self.part.at[wrap(g + k)], self.came.at[i])
            for i, k in enumerate((1, -1, 2))
        ]
        yield 3
        for copy in sends:
            copy.wait_recv()
        there = (self.came[0].astype(F32) + self.came[1].astype(F32)) + self.came[2].astype(F32)
        self.own[...] = (self.part[g].astype(F32) + there).astype(BF16)
        deals = [
            to(at(place, 0, k), self.own.at[wrap(y + k)], self.dealt.at[y]) for k in (1, -1, 2)
        ]
        self.dealt[y] = self.own[y]
        yield 4
        for copy in deals:
            copy.wait_recv()
        cross = to(other_core(), self.dealt.at[pl.ds(2 * (1 - core), 2)], self.out.at[:, core, g])
        self.out[:, core, g] = self.dealt[pl.ds(2 * core, 2)]
        yield 5
        cross.wait_recv()
        mine = self.out.at[:, :, g]
        rounds = [to(beside(k), mine, mine) for k in range(1, SIDE)]
        yield 6
        for copy in rounds:
            copy.wait_recv()
        yield 7


BACK_PLAN = (
    "gdgpu",
    "",
    "d",
    "pg",
    "",
    "pd",
    "ug",
    "",
    "",
    "hdu",
    "o",
    "ghohd",
    "uig",
    "i",
    "ohuih",
    "pogihp",
    "dnho",
    "iup",
    "oppn",
    "iopi",
    "houdp",
)


def back(r):
    place = z, y = spot()
    g = lax.axis_index("dp")
    width = COLS * WIDE
    plan = Plan(BACK_PLAN)
    count = hail(place, wide=True, far=True)
    r.locals = Locals(r.local)
    in_act = r.locals.move(r.act_in, r.act)
    in_down = r.locals.move(r.down_in, r.down)
    in_out = r.locals.move(r.w_out_in, r.w_out)
    r.lows[:, span(y, DEEP)] = r.grad[...].astype(BF16)
    r.dkv[...] = jnp.zeros_like(r.dkv)
    meet(count)
    misc, small = Copies(r.ms, r.mr), Copies(r.ns, r.nr)
    along_y = Along("y", place)

    def cut(ref):
        def pieces(pos, part):
            rows = pl.ds(0, QB) if part is None else pl.ds(part * (QB // 2), QB // 2)
            return [ref.at[rows, span(pos, DEEP)]]

        return pieces

    low_ring = RingGather(misc, along_y, cut(r.lows))
    low_ring.start()
    feeds = [FeedSum(r, name) for name in ("gate", "up", "down")]
    scatter = Scatter(place, r.out_sum, Slabs(r.out_sum.shape[0]), r.halves, r.quarters, r.ss, r.sr)

    def output_flow():
        in_act.wait()
        in_down.wait()
        for i in range(SIDE):
            here = pl.ds(i * QB, QB)
            left = r.act[here, :]
            for n in range(SIDE):
                columns = pl.ds(n * DEEP, DEEP)
                weights = r.down[:, :, :, columns].reshape(left.shape[1], DEEP)
                r.out_sum[here, columns] = nn(left, weights).astype(BF16)
            if i == 1:
                yield -1
        own = r.out_sum.at[span(z, QB), span(y, DEEP)]
        own[...] = (own[...].astype(F32) + r.hidden[...]).astype(BF16)
        yield from scatter.steps()
        for (first, rows), value in scatter.results:
            r.output[pl.ds(first, rows), :] = value.astype(BF16)
        yield 9

    for letter, feed in zip("gud", feeds, strict=True):
        plan.add(letter, feed.steps())
    plan.add("p", output_flow())
    plan.point()
    in_heads = [r.locals.move(r.w_q_in, r.w_q), r.locals.move(r.w_kv_in, r.w_kv)]
    in_x = r.locals.move(r.x_all_in, r.x_all)
    in_raw = r.locals.move(r.raw_in, r.raw)
    plan.point()
    low_ring.relay()
    plan.point()
    plan.point()
    in_out.wait()
    low_ring.finish()

    grad = None
    for n in range(SIDE):
        term = nt(r.lows[:, n * DEEP : (n + 1) * DEEP], out_weights(r, n))
        grad = term if n == 0 else grad + term
    r.gheads[...] = grad.astype(BF16)
    plan.point()

    halo = []
    for j in range(SIDE):
        attend_pair_back(r, jnp.int32(j))
        if j % 2 == 1:
            side = j // 2
            for n in range(2):
                r.halo[n, side] = r.dkv[side, n * QB : (n + 1) * QB].astype(BF16)
                peer = tile_peer(place, n - 2)
                halo.append(misc.to(peer, r.halo.at[n, side], r.halo.at[2 + n, side]))
        plan.point()

    cosine, sine = r.cos[...], -r.sin[...]
    grad_q = jnp.concatenate(
        [turn(r.dq[:, n * WIDE : (n + 1) * WIDE], cosine, sine) for n in range(HEADS // 2)],
        axis=1,
    )
    in_x.wait()
    rms = r.rms[...]

    def weight_grads(target, grads):
        grads = (grads * rms).astype(BF16)
        for n in range(SIDE):
            block = tn(r.x_all[:, n * DEEP : (n + 1) * DEEP], grads).astype(BF16)
            target[n] = block.reshape(*target.shape[1:])

    weight_grads(r.q_grad, grad_q)
    queries = GroupSum(r, place, "q")
    plan.add("h", queries.steps())
    plan.point()

    turned_heads = jnp.transpose(r.heads[...].astype(F32)).astype(BF16)
    for n in range(SIDE):
        block = nn(turned_heads, r.lows[:, n * DEEP : (n + 1) * DEEP]).astype(BF16)
        for k in range(SIDE):
            columns = slice(k * WIDE, (k + 1) * WIDE)
            r.o_grad[n, k] = block[:, columns].reshape(*r.o_grad.shape[2:])
    outs = GroupSum(r, place, "o")
    plan.add("o", outs.steps())
    plan.point()
    plan.point()
    for copy in halo:
        copy.wait_recv()
    for copy in in_heads:
        copy.wait()
    in_raw.wait()
    pieces = []
    for n in range(KVS):
        kv = r.dkv[n, LONGEST:] + (r.halo[2, n].astype(F32) + r.halo[3, n].astype(F32))
        pieces.append(jnp.where(lane(kv.shape) < HS, turn(kv, cosine, sine), kv))
    grad_kv = jnp.concatenate(pieces, axis=1)
    low_q, low_kv = grad_q.astype(BF16), grad_kv.astype(BF16)
    for n in range(SIDE):
        term = nt(low_q, r.w_q[n].reshape(DEEP, -1)) + nt(low_kv, r.w_kv[n].reshape(DEEP, -1))
        r.terms[:, pl.ds(n * DEEP, DEEP)] = term.astype(BF16)
    term_ring = RingScatter(
        misc,
        along_y,
        cut(r.terms),
        [[r.half_terms.at[n]] for n in range(2)],
        [[r.full_terms.at[n]] for n in range(2)],
    )
    term_ring.start()

    weight_grads(r.k_grad, grad_kv)
    keys = GroupSum(r, place, "k")
    plan.add("i", keys.steps())
    plan.point()
    whole = jnp.concatenate([grad_q, grad_kv], axis=1)
    r.stat[...] = row_sums(whole * r.raw[...])
    dots = AxisTotals(place, r.stat, r.slots, r.ts, r.tr)
    plan.point()
    term_ring.relay()
    plan.point()
    plan.point()
    term_ring.wait()
    mean = jnp.transpose(dots.finish())[:, :1] / width
    xhat = r.xt[...].astype(F32) * rms
    summed = term_ring.total()
    gain_sum = jnp.sum(summed * xhat, axis=0, keepdims=True)
    result = r.grad[...] + rms * (gain_row(r.gains, 0) * summed - xhat * mean)
    for k in range(SIDE):
        r.result[k] = result[:, k * WIDE : (k + 1) * WIDE].astype(BF16)
    landing = r.grad_input.at[span(z, QB), :]
    sends = [
        misc.to(at(place, k, 0), r.result.at[wrap(z + k)], landing) for k in (1, -1, 2)
    ]
    landing[...] = r.result[z]

    def gain_flow():
        row = lax.broadcasted_iota(jnp.int32, (8, WIDE), 0)
        gain_two = r.gain_two[...]
        for k in range(SIDE):
            lanes = slice(k * WIDE, (k + 1) * WIDE)
            r.gain_part[k] = jnp.where(row == 0, gain_sum[:, lanes], gain_two[:, lanes])
        moves = [
            small.to(at(place, k, 0), r.gain_part.at[wrap(z + k)], r.gain_z.at[z])
            for k in (1, -1, 2)
        ]
        r.gain_z[z] = r.gain_part[z]
        yield 0
        for copy in moves:
            copy.wait_recv()
        core = lax.axis_index("row")
        mine = r.gain_all.at[core, g]
        mine[...] = (r.gain_z[0] + r.gain_z[1]) + (r.gain_z[2] + r.gain_z[3])
        peers = [other_core()]
        for k in range(1, SIDE):
            peers += [beside(k), {**beside(k), **other_core()}]
        moves = [small.to(peer, mine, mine) for peer in peers]
        yield 1
        for copy in moves:
            copy.wait_recv()
        sums = [r.gain_all[0, k] + r.gain_all[1, k] for k in range(SIDE)]
        r.gain_out[...] = (sums[0] + sums[1]) + (sums[2] + sums[3])
        yield 2

    plan.add("n", gain_flow())
    for _ in range(5):
        plan.point()
    plan.drain("nohigudp")
    for copy in sends:
        copy.wait_recv()
    scatter.finish()
    for group in (misc, small, queries.copies, keys.copies, outs.copies, *(feed.copies for feed in feeds)):
        group.finish()


def call_back(f):
    rows, wide = f.act_out.shape[0], COLS * WIDE
    share, tall, unit = f.gu_grad.shape[2], f.d_grad.shape[2], f.gu_grad.shape[3] // 4
    strip, half, depth = 4 * f.w_out_out.shape[4], f.w_q_out.shape[3], WIDE
    inputs = {
        name: (getattr(f, name + "_out"), VMEM)
        for name in ("xt", "heads", "hidden", "q", "kvs", "rms", "cos", "sin", "start", "gains")
    }
    inputs.update(grad=(f.grad, VMEM), gain_two=(f.gain_two_out, VMEM), act_in=(f.act_out, ANY), down_in=(f.d_out, ANY))
    inputs.update(gu_grad=(f.gu_grad, ANY), d_grad=(f.d_grad, ANY))
    for name in ("x_all", "raw", "w_q", "w_kv", "w_out"):
        inputs[name + "_in"] = (getattr(f, name + "_out"), ANY)
    outs = dict(
        output=(shape((rows, WIDE)), VMEM),
        grad_input=(shape((rows, WIDE)), VMEM),
        gain_out=(shape((8, WIDE), F32), VMEM),
        gate_out=(shape((WIDE, COLS * unit)), ANY),
        up_out=(shape((WIDE, COLS * unit)), ANY),
        down_out=(shape((COLS, SIDE, tall, WIDE)), ANY),
        o_out=(shape((2, 2, SIDE, strip // SIDE, WIDE)), VMEM),
        q_out=(shape((2, 2, SIDE, half // SIDE, HEADS * HS)), VMEM),
        k_out=(shape((2, 2, SIDE, half // SIDE, 2 * KVS * HS)), VMEM),
    )
    scratch = {
        name: pltpu.VMEM(getattr(f, name + "_out").shape, getattr(f, name + "_out").dtype)
        for name in ("x_all", "raw", "w_q", "w_kv", "w_out")
    }
    scratch.update(
        out_sum=pltpu.VMEM((rows, wide), BF16),
        act=pltpu.VMEM(f.act_out.shape, BF16),
        down=pltpu.VMEM(f.d_out.shape, BF16),
        halves=pltpu.VMEM((20, rows // 2, WIDE), BF16),
        quarters=pltpu.VMEM((20, rows // 4, WIDE), BF16),
        lows=pltpu.VMEM((QB, wide), BF16),
        gheads=pltpu.VMEM((QB, HEADS * HS), BF16),
        dq=pltpu.VMEM((QB, HEADS * HS), F32),
        dkv=pltpu.VMEM((KVS, WIN, 2 * HS), F32),
        halo=pltpu.VMEM((4, KVS, QB, 2 * HS), BF16),
        terms=pltpu.VMEM((QB, wide), BF16),
        half_terms=pltpu.VMEM((2, QB // 2, DEEP), BF16),
        full_terms=pltpu.VMEM((2, QB, DEEP), BF16),
        result=pltpu.VMEM((SIDE, QB, WIDE), BF16),
        stat=pltpu.VMEM((8, QB), F32),
        slots=pltpu.VMEM((3, 8, QB), F32),
        ts=dma(3),
        tr=dma(3),
        ss=dma(Scatter.COUNT),
        sr=dma(Scatter.COUNT),
    )
    for name, lead, piece in (
        ("gate", (COLS,), (share, unit)),
        ("up", (COLS,), (share, unit)),
        ("down", (), (tall, wide)),
    ):
        whole = lead + (SIDE,) + piece
        first = lead[0] // 2 if lead else tall // 2
        scratch[name + "_sum"] = pltpu.VMEM(whole, BF16)
        scratch[name + "_came"] = pltpu.VMEM(whole, BF16)
        halves = (first,) + (piece if lead else piece[1:])
        scratch[name + "_half"] = pltpu.VMEM((2,) + halves, BF16)
        scratch[name + "_full"] = pltpu.VMEM((2,) + lead + piece, BF16)
        scratch[name + "_send"] = dma(COLS + 10)
        scratch[name + "_recv"] = dma(COLS + 10)
    for name, piece in (
        ("q", (half, HEADS * HS)),
        ("k", (half, 2 * KVS * HS)),
        ("o", (strip, depth)),
    ):
        small = (SIDE, piece[0] // SIDE, piece[1])
        scratch[name + "_grad"] = pltpu.VMEM((SIDE, SIDE, 2) + piece, BF16)
        scratch[name + "_sum"] = pltpu.VMEM((SIDE, SIDE) + piece, BF16)
        scratch[name + "_half"] = pltpu.VMEM((2, 2) + piece, BF16)
        scratch[name + "_full"] = pltpu.VMEM((2, SIDE) + piece, BF16)
        scratch[name + "_part"] = pltpu.VMEM((SIDE,) + small, BF16)
        scratch[name + "_came"] = pltpu.VMEM((3,) + small, BF16)
        scratch[name + "_own"] = pltpu.VMEM(small, BF16)
        scratch[name + "_dealt"] = pltpu.VMEM(small, BF16)
        scratch[name + "_send"] = dma(16)
        scratch[name + "_recv"] = dma(16)
    scratch.update(
        gain_part=pltpu.VMEM((SIDE, 8, WIDE), F32),
        gain_z=pltpu.VMEM((SIDE, 8, WIDE), F32),
        gain_all=pltpu.VMEM((2, SIDE, 8, WIDE), F32),
        ns=dma(12),
        nr=dma(12),
        ms=dma(16),
        mr=dma(16),
        local=dma(16),
    )
    return launch(back, 2, inputs, outs, scratch)


def finish(gate, up, down, out, queries, pairs, total, grad, gains, *outs):
    gate_o, up_o, down_o, out_o, q_o, k_o, v_o, total_o, grad_o, one_o, two_o = outs
    gate_o[...] = gate[...].astype(F32)
    up_o[...] = up[...].astype(F32)
    down_o[...] = down[...].astype(F32)
    out_o[...] = out[...].astype(F32)
    keys, values = [], []
    for n in range(2):
        q_o[:, n * HEADS * HS : (n + 1) * HEADS * HS] = queries[n].astype(F32)
        whole = pairs[n].astype(F32)
        for kv in range(KVS):
            first = 2 * kv * HS
            keys.append(whole[:, first : first + HS])
            values.append(whole[:, first + HS : first + 2 * HS])
    k_o[...] = jnp.concatenate(keys, axis=1)
    v_o[...] = jnp.concatenate(values, axis=1)
    total_o[...] = total[...]
    grad_o[...] = grad[...].astype(F32)
    one_o[...] = gains[0:1, :]
    two_o[...] = gains[1:2, :]


def call_finish(b):
    arrays = (
        b.gate_out,
        b.up_out,
        b.down_out.reshape(-1, WIDE),
        b.o_out.reshape(-1, WIDE),
        b.q_out.reshape(2, WIDE, HEADS * HS),
        b.k_out.reshape(2, WIDE, 2 * KVS * HS),
        b.output,
        b.grad_input,
    )
    gate, up, down, out, queries, pairs, total, grad = arrays

    def cut(array):
        rows, columns = array.shape[-2] // 2, array.shape[-1]
        if len(array.shape) == 3:
            return pl.BlockSpec((array.shape[0], rows, columns), lambda i: (0, i, 0))
        return pl.BlockSpec((rows, columns), lambda i: (i, 0))

    small = pl.BlockSpec((1, WIDE), lambda i: (0, 0))
    outs = (
        shape(gate.shape, F32),
        shape(up.shape, F32),
        shape(down.shape, F32),
        shape(out.shape, F32),
        shape((WIDE, 2 * HEADS * HS), F32),
        shape((WIDE, 2 * KVS * HS), F32),
        shape((WIDE, 2 * KVS * HS), F32),
        shape(total.shape),
        shape(grad.shape, F32),
    )
    return pl.pallas_call(
        finish,
        grid=(2,),
        out_shape=outs + (shape((1, WIDE), F32),) * 2,
        in_specs=[cut(a) for a in arrays] + [pl.BlockSpec((8, WIDE), lambda i: (0, 0))],
        out_specs=tuple(cut(a) for a in outs) + (small, small),
        compiler_params=pltpu.CompilerParams(vmem_limit_bytes=60 * MIB),
        name="finish",
    )(*arrays, b.gain_out)


def on_device(
    block_input,
    gain_attn,
    w_query,
    w_key,
    w_value,
    w_out,
    gain_mlp,
    w_gate,
    w_up,
    w_down,
    lengths,
    cotangent,
):
    f = call_ahead(
        block_input,
        gain_attn,
        gain_mlp,
        cotangent,
        w_query,
        w_key,
        w_value,
        w_out,
        w_gate,
        w_up,
        w_down,
        lengths,
    )
    b = call_back(f)
    gate, up, down, out, query, key, value, output, grad_input, one, two = call_finish(b)
    return (
        output,
        grad_input,
        one.reshape(WIDE),
        query,
        key,
        value,
        out,
        two.reshape(WIDE),
        gate,
        up,
        down,
    )


def solution(mesh):
    in_specs = (
        P(("dp", "row"), "col"),
        P("col"),
        P("col", "row"),
        P("col", "row"),
        P("col", "row"),
        P("row", "col"),
        P("col"),
        P("col", "row"),
        P("col", "row"),
        P("row", "col"),
        P("dp", None),
        P(("dp", "row"), "col"),
    )
    out_specs = (
        P(("dp", "row"), "col"),
        P(("dp", "row"), "col"),
        P("col"),
        P("col", "row"),
        P("col", "row"),
        P("col", "row"),
        P("row", "col"),
        P("col"),
        P("col", "row"),
        P("col", "row"),
        P("row", "col"),
    )
    return jax.shard_map(
        on_device, mesh=mesh, in_specs=in_specs, out_specs=out_specs, check_vma=False
    )
```
